32 devices in a mesh: section: 2 (over x), chan: 4 (over z), batch: 4 (over y, core).
Axes of the slice: x: 2, y: 2, z: 4, core: 2. Of those that a mesh axis runs over, the one named last changes fastest.
Arguments:
- images: bfloat16 [2, 4, 4, 256, 1024], P('section', 'batch', 'chan'), may hold values from -12 to 12
- w_early: bfloat16 [1024, 2048], replicated, may hold values from -0.1875 to 0.1875
- gain_early: float32 [2048], replicated, may hold values from 0.5 to 1.5
- bias_early: float32 [2048], replicated, may hold values from -0.5 to 0.5
- w_late: bfloat16 [2048, 8192], P(None, 'chan'), may hold values from -0.125 to 0.125
- gain_late: float32 [8192], P('chan'), may hold values from 0.5 to 1.5
- bias_late: float32 [8192], P('chan'), may hold values from -0.5 to 0.5
- cotangent: bfloat16 [2, 16, 256, 8192], P('section', 'batch', None, 'chan'), may hold values from -6 to 6
Outputs:
- late_out: bfloat16 [2, 16, 256, 8192], P('section', 'batch', None, 'chan')
- grad_late: float32 [2048, 8192], P(None, 'chan')
- grad_early: float32 [1024, 2048], P(('section', 'chan', 'batch'))
The draws below stay inside these ranges and needn't reach their ends.
All inputs are finite; a program needn't handle non-finite values.
Results may differ from the reference program's by a relative error of at most 0.024.
Values may be sent and summed in bfloat16 or wider, within the bound.
A program may use at most 192 MiB of HBM per device.

```python
import jax
import jax.numpy as jnp
from jax import lax

E = 1024
A = 2048
L = 8192
PIX = 256
IMG_DEV = 1
IMAGES = 16
MICRO = 2
N_CHAN = 4
N_BATCH = 4


def draw_images(key, part):
    key = jax.random.fold_in(key, 11)
    key_base, key_scale, key_shared, key_own, key_rate = jax.random.split(key, 5)
    shape = (MICRO, N_BATCH, N_CHAN * IMG_DEV, PIX, E)
    batch_pos = jnp.arange(N_BATCH, dtype=jnp.float32).reshape(1, N_BATCH, 1, 1, 1)
    chan_pos = (jnp.arange(N_CHAN * IMG_DEV, dtype=jnp.float32) // IMG_DEV).reshape(1, 1, N_CHAN * IMG_DEV, 1, 1)
    order = (chan_pos * N_BATCH + batch_pos) / (N_CHAN * N_BATCH - 1)
    image_scale = jnp.exp(jax.random.uniform(key_scale, (MICRO, N_BATCH, N_CHAN * IMG_DEV, 1, 1), jnp.float32, -0.8, 0.8))
    shared = jax.random.uniform(key_shared, (1, 1, 1, 1, E), jnp.float32, -1.0, 1.0)
    own = 0.3 * jax.random.normal(key_own, (MICRO, N_BATCH, N_CHAN * IMG_DEV, 1, E), jnp.float32)
    base = jnp.clip(jax.random.normal(key_base, shape, jnp.float32), -4.0, 4.0)
    rate = jax.random.uniform(key_rate, (), jnp.float32, 1.0986123, 1.6094379)
    values = 0.5 * (base + shared + own) * jnp.exp(order * rate) * image_scale
    return jnp.clip(values, -12.0, 12.0).astype(jnp.bfloat16)


def block_scale(stream_key, dims, cuts, least, top_value):
    loudness, own = 1.0, jax.random.fold_in(stream_key, 6)
    for position, shards_of in cuts:
        heights = jnp.exp(jax.random.uniform(jax.random.fold_in(own, position), (shards_of,), jnp.float32, least / len(cuts), top_value / len(cuts)))
        loudness = loudness * jnp.repeat(heights, dims[position] // shards_of).reshape([-1 if axis == position else 1 for axis in range(len(dims))])
    return loudness


def centred(key, extent, width, bound, pieces=(), kind=jnp.bfloat16):
    level = block_scale(key, extent, pieces, -0.22, 0.18) if pieces else 1.0
    result = jax.random.normal(key, extent, jnp.float32) * width * level
    return jnp.minimum(jnp.maximum(result, -bound), bound).astype(kind)


def setup_inputs(seed: int = 0) -> dict:
    arg_keys = jax.random.split(jax.random.key(seed), 9)
    images = draw_images(jax.random.fold_in(arg_keys[8], 71), 0)
    w_early = centred(arg_keys[1], (E, A), E ** -0.5, 0.1875)
    gain_early = jnp.clip(jax.random.uniform(arg_keys[2], (A,), jnp.float32, 0.5, 1.5), 0.5, 1.5)
    bias_early = jnp.clip(jax.random.uniform(arg_keys[3], (A,), jnp.float32, -0.5, 0.5), -0.5, 0.5)
    w_late = centred(arg_keys[4], (A, L), A ** -0.5, 0.125, ((1, 4),))
    gain_late = jnp.clip(0.5 + 1.0 * jax.random.uniform(arg_keys[5], (L,), jnp.float32) ** block_scale(arg_keys[5], (L,), ((0, 4),), -0.2, 0.2), 0.5, 1.5)
    bias_late = jnp.clip(jax.random.uniform(arg_keys[6], (L,), jnp.float32, -0.5, 0.5) * block_scale(arg_keys[6], (L,), ((0, 4),), -0.4, 0.0), -0.5, 0.5)
    cotangent = centred(arg_keys[7], (MICRO, IMAGES, PIX, L), 1.0, 6.0, ((0, 2), (1, 4), (3, 4)))
    return dict(images=images, w_early=w_early, gain_early=gain_early, bias_early=bias_early, w_late=w_late, gain_late=gain_late, bias_late=bias_late, cotangent=cotangent)


def smooth_gate(values):
    return values * jax.nn.sigmoid(values)

def smooth_slope(values):
    sig = jax.nn.sigmoid(values)
    return sig * (1.0 + values * (1.0 - sig))

def norm_forward(values, gain, bias):
    count = values.shape[0]
    mean = lax.optimization_barrier(jnp.sum(values, 0)) / count
    rstd = lax.rsqrt(lax.optimization_barrier(jnp.sum(values * values, 0)) / count - mean * mean + 1e-05)
    normed = (values - mean) * rstd
    return (normed, rstd, normed * gain + bias)

def norm_backward(grad, normed, rstd, gain):
    count = grad.shape[0]
    first = lax.optimization_barrier(jnp.sum(grad, 0)) / count
    second = lax.optimization_barrier(jnp.sum(grad * normed, 0)) / count
    return gain * rstd * (grad - first - normed * second)

def reference(images, w_early, gain_early, bias_early, w_late, gain_late, bias_late, cotangent):
    micro = images.shape[0]
    width_in = images.shape[4]
    width_mid = w_early.shape[1]
    width_out = w_late.shape[1]
    group = width_out // N_CHAN
    image_total = images.shape[1] * images.shape[2]
    outputs = []
    grad_late = jnp.zeros((width_mid, width_out), jnp.float32)
    grad_early = jnp.zeros((width_in, width_mid), jnp.float32)
    for index in range(micro):
        flat_in = images[index].reshape(-1, width_in)
        raw = jnp.dot(flat_in, w_early, preferred_element_type=jnp.float32).astype(jnp.bfloat16)
        normed_e, rstd_e, pre_e = norm_forward(raw.astype(jnp.float32), gain_early, bias_early)
        act = smooth_gate(pre_e).astype(jnp.bfloat16)
        hidden = jnp.dot(act, w_late, preferred_element_type=jnp.float32)
        normed_l, rstd_l, pre_l = norm_forward(hidden, gain_late, bias_late)
        outputs.append(smooth_gate(pre_l).astype(jnp.bfloat16).reshape(image_total, images.shape[3], width_out))
        grad_y = cotangent[index].reshape(-1, width_out).astype(jnp.float32) * smooth_slope(pre_l)
        grad_h = norm_backward(grad_y, normed_l, rstd_l, gain_late).astype(jnp.bfloat16)
        grad_late = grad_late + jnp.dot(act.T, grad_h, preferred_element_type=jnp.float32)
        grad_act = jnp.zeros((flat_in.shape[0], width_mid), jnp.float32)
        for block in range(N_CHAN):
            part = jnp.dot(grad_h[:, block * group:(block + 1) * group], w_late[:, block * group:(block + 1) * group].T, preferred_element_type=jnp.float32)
            grad_act = grad_act + part.astype(jnp.bfloat16).astype(jnp.float32)
        grad_pre = grad_act * smooth_slope(pre_e)
        grad_raw = norm_backward(grad_pre, normed_e, rstd_e, gain_early).astype(jnp.bfloat16)
        grad_early = grad_early + jnp.dot(flat_in.T, grad_raw, preferred_element_type=jnp.float32)
    return (jnp.stack(outputs), grad_late, grad_early)
```

```python
import functools

import jax
import jax.numpy as jnp
from jax import lax
from jax.experimental import pallas as pl
from jax.experimental.pallas import tpu as pltpu
from jax.sharding import PartitionSpec as P

MESH = pl.DeviceIdType.MESH


def smooth_gate(values):
    return values * jax.nn.sigmoid(values)


def smooth_slope(values):
    sig = jax.nn.sigmoid(values)
    return sig * (1.0 + values * (1.0 - sig))


def sums_kernel(n, x_ref, o_ref, buf, send_sem, recv_sem):
    me = lax.axis_index("batch")
    peers = [lax.rem(me + d, n) for d in range(1, n)]
    barrier = pltpu.get_barrier_semaphore()
    for peer in peers:
        pl.semaphore_signal(barrier, inc=1, device_id={"batch": peer}, device_id_type=MESH)
    buf[me] = x_ref[...]
    pl.semaphore_wait(barrier, n - 1)
    copies = []
    for peer in peers:
        copy = pltpu.make_async_remote_copy(
            src_ref=x_ref,
            dst_ref=buf.at[me],
            send_sem=send_sem.at[peer],
            recv_sem=recv_sem.at[me],
            device_id={"batch": peer},
            device_id_type=MESH,
        )
        copy.start()
        copies.append(copy)
    for peer in peers:
        pltpu.make_async_remote_copy(
            src_ref=x_ref,
            dst_ref=buf.at[peer],
            send_sem=send_sem.at[peer],
            recv_sem=recv_sem.at[peer],
            device_id={"batch": peer},
            device_id_type=MESH,
        ).wait_recv()
    total = buf[0]
    for k in range(1, n):
        total = total + buf[k]
    o_ref[...] = total
    for copy in copies:
        copy.wait_send()


def batch_sums(one, two, collective_id):
    n = lax.axis_size("batch")
    width = one.shape[0]
    x = jnp.concatenate([one, two]).reshape(-1, 128)
    out = pl.pallas_call(
        functools.partial(sums_kernel, n),
        out_shape=jax.ShapeDtypeStruct(x.shape, x.dtype),
        in_specs=[pl.BlockSpec(memory_space=pltpu.VMEM)],
        out_specs=pl.BlockSpec(memory_space=pltpu.VMEM),
        scratch_shapes=[
            pltpu.VMEM((n,) + x.shape, x.dtype),
            pltpu.SemaphoreType.DMA((n,)),
            pltpu.SemaphoreType.DMA((n,)),
        ],
        compiler_params=pltpu.CompilerParams(collective_id=collective_id, has_side_effects=True),
        name=f"batch_sums_{collective_id}",
    )(x)
    out = out.reshape(2, width)
    return out[0], out[1]


def body(images, w_early, gain_early, bias_early, w_late, gain_late, bias_late, cotangent):
    width_in = images.shape[-1]
    width_mid = w_early.shape[1]
    width_out = w_late.shape[1]
    batch_count = lax.axis_size("batch")
    own = images.reshape(-1, width_in)
    flat_in = lax.all_gather(own, "chan", axis=0, tiled=True)
    total_rows = flat_in.shape[0] * batch_count

    raw = jnp.dot(flat_in, w_early, preferred_element_type=jnp.float32).astype(jnp.bfloat16)
    raw_f = raw.astype(jnp.float32)
    sum_one, sum_two = batch_sums(jnp.sum(raw_f, 0), jnp.sum(raw_f * raw_f, 0), 0)
    mean_e = sum_one / total_rows
    rstd_e = lax.rsqrt(sum_two / total_rows - mean_e * mean_e + 1e-05)
    normed_e = (raw_f - mean_e) * rstd_e
    pre_e = normed_e * gain_early + bias_early
    act = smooth_gate(pre_e).astype(jnp.bfloat16)

    late = jnp.dot(act, w_late, preferred_element_type=jnp.float32)
    late_one, late_two = batch_sums(jnp.sum(late, 0), jnp.sum(late * late, 0), 1)
    mean_l = late_one / total_rows
    rstd_l = lax.rsqrt(late_two / total_rows - mean_l * mean_l + 1e-05)
    normed_l = (late - mean_l) * rstd_l
    pre_l = normed_l * gain_late + bias_late
    late_out = smooth_gate(pre_l).astype(jnp.bfloat16).reshape(cotangent.shape)
    grad_y = cotangent.reshape(-1, width_out).astype(jnp.float32) * smooth_slope(pre_l)
    back_one, back_two = batch_sums(jnp.sum(grad_y, 0), jnp.sum(grad_y * normed_l, 0), 2)
    grad_h = (
        gain_late * rstd_l * (grad_y - back_one / total_rows - normed_l * (back_two / total_rows))
    ).astype(jnp.bfloat16)

    grad_act = lax.dot_general(
        grad_h, w_late, (((1,), (1,)), ((), ())), preferred_element_type=jnp.float32
    )
    grad_pre = grad_act * smooth_slope(pre_e)
    early_one, early_two = batch_sums(jnp.sum(grad_pre, 0), jnp.sum(grad_pre * normed_e, 0), 3)
    grad_raw = (
        gain_early
        * rstd_e
        * (grad_pre - early_one / total_rows - normed_e * (early_two / total_rows))
    ).astype(jnp.bfloat16)
    part_early = lax.dot_general(
        flat_in, grad_raw, (((0,), (0,)), ((), ())), preferred_element_type=jnp.float32
    ).astype(jnp.bfloat16)
    grad_early = lax.psum_scatter(
        part_early, ("section", "chan", "batch"), scatter_dimension=0, tiled=True
    ).astype(jnp.float32)

    part_late = lax.dot_general(
        act, grad_h, (((0,), (0,)), ((), ())), preferred_element_type=jnp.float32
    ).astype(jnp.bfloat16)
    grad_late = lax.psum(part_late, ("section", "batch")).astype(jnp.float32)
    return (late_out, grad_late, grad_early)


def solution(mesh):
    return jax.shard_map(
        body,
        mesh=mesh,
        in_specs=(
            P("section", "batch", "chan", None, None),
            P(),
            P(),
            P(),
            P(None, "chan"),
            P("chan"),
            P("chan"),
            P("section", "batch", None, "chan"),
        ),
        out_specs=(
            P("section", "batch", None, "chan"),
            P(None, "chan"),
            P(("section", "chan", "batch"), None),
        ),
        check_vma=False,
    )
```

```python
import functools

import jax
import jax.numpy as jnp
from jax import lax
from jax.experimental import pallas as pl
from jax.experimental.pallas import tpu as pltpu
from jax.sharding import PartitionSpec as P

MESH = pl.DeviceIdType.MESH


def smooth_gate(values):
    return values * jax.nn.sigmoid(values)


def smooth_slope(values):
    sig = jax.nn.sigmoid(values)
    return sig * (1.0 + values * (1.0 - sig))


def sums_kernel(n, x_ref, o_ref, buf, send_sem, recv_sem):
    me = lax.axis_index("batch")
    peers = [lax.rem(me + d, n) for d in range(1, n)]
    barrier = pltpu.get_barrier_semaphore()
    for peer in peers:
        pl.semaphore_signal(barrier, inc=1, device_id={"batch": peer}, device_id_type=MESH)
    buf[me] = x_ref[...]
    pl.semaphore_wait(barrier, n - 1)
    copies = []
    for peer in peers:
        copy = pltpu.make_async_remote_copy(
            src_ref=x_ref,
            dst_ref=buf.at[me],
            send_sem=send_sem.at[peer],
            recv_sem=recv_sem.at[me],
            device_id={"batch": peer},
            device_id_type=MESH,
        )
        copy.start()
        copies.append(copy)
    for peer in peers:
        pltpu.make_async_remote_copy(
            src_ref=x_ref,
            dst_ref=buf.at[peer],
            send_sem=send_sem.at[peer],
            recv_sem=recv_sem.at[peer],
            device_id={"batch": peer},
            device_id_type=MESH,
        ).wait_recv()
    total = buf[0]
    for k in range(1, n):
        total = total + buf[k]
    o_ref[...] = total
    for copy in copies:
        copy.wait_send()


def batch_sums(one, two, collective_id):
    n = lax.axis_size("batch")
    width = one.shape[0]
    x = jnp.concatenate([one, two]).reshape(-1, 128)
    out = pl.pallas_call(
        functools.partial(sums_kernel, n),
        out_shape=jax.ShapeDtypeStruct(x.shape, x.dtype),
        in_specs=[pl.BlockSpec(memory_space=pltpu.VMEM)],
        out_specs=pl.BlockSpec(memory_space=pltpu.VMEM),
        scratch_shapes=[
            pltpu.VMEM((n,) + x.shape, x.dtype),
            pltpu.SemaphoreType.DMA((n,)),
            pltpu.SemaphoreType.DMA((n,)),
        ],
        compiler_params=pltpu.CompilerParams(collective_id=collective_id, has_side_effects=True),
        name=f"batch_sums_{collective_id}",
    )(x)
    out = out.reshape(2, width)
    return out[0], out[1]


def meet(groups):
    barrier = pltpu.get_barrier_semaphore()
    for device in groups:
        pl.semaphore_signal(barrier, inc=1, device_id=device, device_id_type=MESH)
    pl.semaphore_wait(barrier, len(groups))


def remote(src, dst, send_sem, recv_sem, device):
    return pltpu.make_async_remote_copy(
        src_ref=src,
        dst_ref=dst,
        send_sem=send_sem,
        recv_sem=recv_sem,
        device_id=device,
        device_id_type=MESH,
    )


def others(axis, n):
    me = lax.axis_index(axis)
    return [lax.rem(me + d, n) for d in range(1, n)]


def exchange(n, buf, send_sem, recv_sem):
    me = lax.axis_index("batch")
    peers = others("batch", n)
    for peer in peers:
        remote(buf.at[me], buf.at[me], send_sem.at[peer], recv_sem.at[me], {"batch": peer}).start()
    for peer in peers:
        remote(
            buf.at[peer], buf.at[peer], send_sem.at[peer], recv_sem.at[peer], {"batch": peer}
        ).wait()
    total = buf[0]
    for k in range(1, n):
        total = total + buf[k]
    return total


def early_kernel(n_chan, n_batch, x_ref, w_ref, x_out, raw_out, sum_out, held, buf,
                 up_send, up_recv, down_send, down_recv, sum_send, sum_recv):
    z = lax.axis_index("chan")
    me = lax.axis_index("batch")
    rows = x_ref.shape[0]
    meet([{"chan": p} for p in others("chan", n_chan)]
         + [{"batch": p} for p in others("batch", n_batch)])
    held[z] = x_ref[...]

    def up(block):
        return remote(held.at[block], held.at[block], up_send.at[block], up_recv.at[block],
                      {"chan": lax.rem(z + 1, n_chan)})

    def down(block):
        return remote(held.at[block], held.at[block], down_send.at[block], down_recv.at[block],
                      {"chan": lax.rem(z + n_chan - 1, n_chan)})

    @pl.when(z < n_chan - 1)
    def _():
        up(z).start()

    @pl.when(z > 0)
    def _():
        down(z).start()

    def multiply(block):
        at = pl.ds(pl.multiple_of(block * rows, rows), rows)
        width = w_ref.shape[1]
        step = min(width, 512)

        @pl.loop(0, width // step)
        def _(i):
            cols = pl.ds(pl.multiple_of(i * step, step), step)
            raw = jnp.dot(
                held[block], w_ref[:, cols], preferred_element_type=jnp.float32
            ).astype(jnp.bfloat16)
            raw_out[at, cols] = raw
            raw = raw.astype(jnp.float32)
            buf[me, 0:1, cols] += jnp.sum(raw, 0, keepdims=True)
            buf[me, 1:2, cols] += jnp.sum(raw * raw, 0, keepdims=True)

    buf[me] = jnp.zeros(buf.shape[1:], buf.dtype)
    multiply(z)
    for i in range(1, n_chan):
        below, above = z - i, z + i

        @pl.when(below >= 0)
        def _():
            up(below).wait_recv()

            @pl.when(z < n_chan - 1)
            def _():
                up(below).start()

        @pl.when(above < n_chan)
        def _():
            down(above).wait_recv()

            @pl.when(z > 0)
            def _():
                down(above).start()

        @pl.when(below >= 0)
        def _():
            multiply(below)

        @pl.when(above < n_chan)
        def _():
            multiply(above)

    sum_out[...] = exchange(n_batch, buf, sum_send, sum_recv)
    x_out[...] = held[...].reshape(x_out.shape)
    for block in range(n_chan):
        @pl.when(jnp.logical_and(block <= z, z < n_chan - 1))
        def _():
            up(block).wait_send()

        @pl.when(jnp.logical_and(block >= z, z > 0))
        def _():
            down(block).wait_send()


def early_forward(x, w, collective_id):
    n_chan, n_batch = lax.axis_size("chan"), lax.axis_size("batch")
    rows, width_in = x.shape
    width = w.shape[1]
    return pl.pallas_call(
        functools.partial(early_kernel, n_chan, n_batch),
        out_shape=(
            jax.ShapeDtypeStruct((n_chan * rows, width_in), x.dtype),
            jax.ShapeDtypeStruct((n_chan * rows, width), x.dtype),
            jax.ShapeDtypeStruct((8, width), jnp.float32),
        ),
        in_specs=[pl.BlockSpec(memory_space=pltpu.VMEM)] * 2,
        out_specs=[pl.BlockSpec(memory_space=pltpu.VMEM)] * 3,
        scratch_shapes=[
            pltpu.VMEM((n_chan, rows, width_in), x.dtype),
            pltpu.VMEM((n_batch, 8, width), jnp.float32),
        ]
        + [pltpu.SemaphoreType.DMA((n_chan,))] * 4
        + [pltpu.SemaphoreType.DMA((n_batch,))] * 2,
        compiler_params=pltpu.CompilerParams(
            collective_id=collective_id, has_side_effects=True, vmem_limit_bytes=56 * 2**20
        ),
        name="early_forward",
    )(x, w)


def early_grad_kernel(n_sec, n_chan, n_batch, x_ref, g_ref, o_ref, part, pair, mine, low, high, last,
                      pair_send, pair_recv, low_send, low_recv, high_send, high_recv,
                      last_send, last_recv):
    s, z, b = lax.axis_index("section"), lax.axis_index("chan"), lax.axis_index("batch")
    n_y = n_batch // 2
    y, core = b // 2, lax.rem(b, 2)
    sibling = {"batch": y * 2 + 1 - core}
    plane = [
        (lax.rem(s + i, n_sec), lax.rem(y + j, n_y))
        for i in range(n_sec) for j in range(n_y) if i + j > 0
    ]
    meet([sibling] + [{"chan": p} for p in others("chan", n_chan)]
         + [{"section": p, "batch": q * 2 + core} for p, q in plane])
    rows, width = o_ref.shape
    span = rows * n_batch
    step = min(width, 512)

    order = []
    for i in range(n_chan // 2):
        order += [i, n_chan - 1 - i]
    for d in order:
        lhs = jnp.concatenate(
            [x_ref[:, (k * n_chan + d) * span:(k * n_chan + d + 1) * span] for k in range(n_sec)], 1
        ).T

        @pl.loop(0, width // step)
        def _(i):
            cols = pl.ds(pl.multiple_of(i * step, step), step)
            block = jnp.dot(lhs, g_ref[:, cols], preferred_element_type=jnp.float32)
            part[d, :, :, :, :, cols] = block.reshape(n_sec, n_y, 2, rows, step).astype(jnp.bfloat16)

        remote(part.at[d, :, :, 1 - core], pair.at[d], pair_send.at[d], pair_recv.at[d],
               sibling).start()

    def from_pair(d):
        remote(part.at[d, :, :, 1 - core], pair.at[d], pair_send.at[d], pair_recv.at[d],
               sibling).wait_recv()
        mine[d] = (
            part[d, :, :, core].astype(jnp.float32) + pair[d].astype(jnp.float32)
        ).astype(jnp.bfloat16)

    def lower(d):
        return remote(mine.at[d], low.at[d], low_send.at[d], low_recv.at[d],
                      {"chan": lax.rem(z + n_chan - 1, n_chan)})

    def upper(d):
        return remote(mine.at[d], high.at[d], high_send.at[d], high_recv.at[d],
                      {"chan": lax.rem(z + 1, n_chan)})

    def add(d, arrived):
        mine[d] = (mine[d].astype(jnp.float32) + arrived[d].astype(jnp.float32)).astype(jnp.bfloat16)

    for d in order:
        from_pair(d)

        @pl.when(jnp.logical_and(z == n_chan - 1, d < z))
        def _():
            lower(d).start()

        @pl.when(jnp.logical_and(z == 0, d > z))
        def _():
            upper(d).start()

    for i in range(n_chan):
        d, e = i, n_chan - 1 - i

        @pl.when(jnp.logical_and(z < n_chan - 1, d <= z))
        def _():
            lower(d).wait_recv()
            add(d, low)

            @pl.when(d < z)
            def _():
                lower(d).start()

        @pl.when(jnp.logical_and(z > 0, e >= z))
        def _():
            upper(e).wait_recv()
            add(e, high)

            @pl.when(e > z)
            def _():
                upper(e).start()

    slot = s * n_y + y
    for p, q in plane:
        remote(mine.at[z, p, q], last.at[slot], last_send.at[p * n_y + q], last_recv.at[slot],
               {"section": p, "batch": q * 2 + core}).start()
    total = mine[z, s, y].astype(jnp.float32)
    for p, q in plane:
        there = p * n_y + q
        remote(mine.at[z, p, q], last.at[there], last_send.at[there], last_recv.at[there],
               {"section": p, "batch": q * 2 + core}).wait()
        total = total + last[there].astype(jnp.float32)
    o_ref[...] = total
    for d in range(n_chan):
        remote(part.at[d, :, :, 1 - core], pair.at[d], pair_send.at[d], pair_recv.at[d],
               sibling).wait_send()

        @pl.when(d < z)
        def _():
            lower(d).wait_send()

        @pl.when(d > z)
        def _():
            upper(d).wait_send()


def early_gradient(x, g, collective_id):
    n_sec, n_chan, n_batch = (lax.axis_size(a) for a in ("section", "chan", "batch"))
    n_y = n_batch // 2
    width = g.shape[1]
    rows = x.shape[1] // (n_sec * n_chan * n_batch)
    quarter = (n_chan, n_sec, n_y, rows, width)
    return pl.pallas_call(
        functools.partial(early_grad_kernel, n_sec, n_chan, n_batch),
        out_shape=jax.ShapeDtypeStruct((rows, width), jnp.float32),
        in_specs=[pl.BlockSpec(memory_space=pltpu.VMEM)] * 2,
        out_specs=pl.BlockSpec(memory_space=pltpu.VMEM),
        scratch_shapes=[pltpu.VMEM((n_chan, n_sec, n_y, 2, rows, width), jnp.bfloat16)]
        + [pltpu.VMEM(quarter, jnp.bfloat16)] * 4
        + [pltpu.VMEM((n_sec * n_y, rows, width), jnp.bfloat16)]
        + [pltpu.SemaphoreType.DMA((n_chan,))] * 6
        + [pltpu.SemaphoreType.DMA((n_sec * n_y,))] * 2,
        compiler_params=pltpu.CompilerParams(
            collective_id=collective_id, has_side_effects=True, vmem_limit_bytes=56 * 2**20
        ),
        name="early_gradient",
    )(x, g)


def body(images, w_early, gain_early, bias_early, w_late, gain_late, bias_late, cotangent):
    width_in = images.shape[-1]
    width_mid = w_early.shape[1]
    width_out = w_late.shape[1]
    batch_count = lax.axis_size("batch")
    own = images.reshape(-1, width_in)
    flat_in, raw, sums_e = early_forward(own, w_early, 0)
    total_rows = flat_in.shape[0] * batch_count

    raw_f = raw.astype(jnp.float32)
    sum_one, sum_two = sums_e[0], sums_e[1]
    mean_e = sum_one / total_rows
    rstd_e = lax.rsqrt(sum_two / total_rows - mean_e * mean_e + 1e-05)
    normed_e = (raw_f - mean_e) * rstd_e
    pre_e = normed_e * gain_early + bias_early
    act = smooth_gate(pre_e).astype(jnp.bfloat16)

    late = jnp.dot(act, w_late, preferred_element_type=jnp.float32)
    late_one, late_two = batch_sums(jnp.sum(late, 0), jnp.sum(late * late, 0), 1)
    mean_l = late_one / total_rows
    rstd_l = lax.rsqrt(late_two / total_rows - mean_l * mean_l + 1e-05)
    normed_l = (late - mean_l) * rstd_l
    pre_l = normed_l * gain_late + bias_late
    late_out = smooth_gate(pre_l).astype(jnp.bfloat16).reshape(cotangent.shape)
    grad_y = cotangent.reshape(-1, width_out).astype(jnp.float32) * smooth_slope(pre_l)
    back_one, back_two = batch_sums(jnp.sum(grad_y, 0), jnp.sum(grad_y * normed_l, 0), 2)
    grad_h = (
        gain_late * rstd_l * (grad_y - back_one / total_rows - normed_l * (back_two / total_rows))
    ).astype(jnp.bfloat16)

    part_late = lax.dot_general(
        act, grad_h, (((0,), (0,)), ((), ())), preferred_element_type=jnp.float32
    ).astype(jnp.bfloat16)
    part_late, grad_h = lax.optimization_barrier((part_late, grad_h))
    grad_late = lax.psum(part_late, ("section", "batch")).astype(jnp.float32)

    grad_act = lax.dot_general(
        grad_h, w_late, (((1,), (1,)), ((), ())), preferred_element_type=jnp.float32
    )
    grad_pre = grad_act * smooth_slope(pre_e)
    early_one, early_two = batch_sums(jnp.sum(grad_pre, 0), jnp.sum(grad_pre * normed_e, 0), 3)
    grad_raw = (
        gain_early
        * rstd_e
        * (grad_pre - early_one / total_rows - normed_e * (early_two / total_rows))
    ).astype(jnp.bfloat16)
    grad_early = early_gradient(flat_in, grad_raw, 4)
    return (late_out, grad_late, grad_early)


def solution(mesh):
    return jax.shard_map(
        body,
        mesh=mesh,
        in_specs=(
            P("section", "batch", "chan", None, None),
            P(),
            P(),
            P(),
            P(None, "chan"),
            P("chan"),
            P("chan"),
            P("section", "batch", None, "chan"),
        ),
        out_specs=(
            P("section", "batch", None, "chan"),
            P(None, "chan"),
            P(("section", "chan", "batch"), None),
        ),
        check_vma=False,
    )
```

```python
import functools

import jax
import jax.numpy as jnp
from jax import lax
from jax.experimental import pallas as pl
from jax.experimental.pallas import tpu as pltpu
from jax.sharding import PartitionSpec as P

MESH = pl.DeviceIdType.MESH


def smooth_gate(values):
    return values * jax.nn.sigmoid(values)


def smooth_slope(values):
    sig = jax.nn.sigmoid(values)
    return sig * (1.0 + values * (1.0 - sig))


def sums_kernel(n, x_ref, o_ref, buf, send_sem, recv_sem):
    me = lax.axis_index("batch")
    peers = [lax.rem(me + d, n) for d in range(1, n)]
    barrier = pltpu.get_barrier_semaphore()
    for peer in peers:
        pl.semaphore_signal(barrier, inc=1, device_id={"batch": peer}, device_id_type=MESH)
    buf[me] = x_ref[...]
    pl.semaphore_wait(barrier, n - 1)
    copies = []
    for peer in peers:
        copy = pltpu.make_async_remote_copy(
            src_ref=x_ref,
            dst_ref=buf.at[me],
            send_sem=send_sem.at[peer],
            recv_sem=recv_sem.at[me],
            device_id={"batch": peer},
            device_id_type=MESH,
        )
        copy.start()
        copies.append(copy)
    for peer in peers:
        pltpu.make_async_remote_copy(
            src_ref=x_ref,
            dst_ref=buf.at[peer],
            send_sem=send_sem.at[peer],
            recv_sem=recv_sem.at[peer],
            device_id={"batch": peer},
            device_id_type=MESH,
        ).wait_recv()
    total = buf[0]
    for k in range(1, n):
        total = total + buf[k]
    o_ref[...] = total
    for copy in copies:
        copy.wait_send()


def batch_sums(one, two, collective_id):
    n = lax.axis_size("batch")
    width = one.shape[0]
    x = jnp.concatenate([one, two]).reshape(-1, 128)
    out = pl.pallas_call(
        functools.partial(sums_kernel, n),
        out_shape=jax.ShapeDtypeStruct(x.shape, x.dtype),
        in_specs=[pl.BlockSpec(memory_space=pltpu.VMEM)],
        out_specs=pl.BlockSpec(memory_space=pltpu.VMEM),
        scratch_shapes=[
            pltpu.VMEM((n,) + x.shape, x.dtype),
            pltpu.SemaphoreType.DMA((n,)),
            pltpu.SemaphoreType.DMA((n,)),
        ],
        compiler_params=pltpu.CompilerParams(collective_id=collective_id, has_side_effects=True),
        name=f"batch_sums_{collective_id}",
    )(x)
    out = out.reshape(2, width)
    return out[0], out[1]


def meet(groups):
    barrier = pltpu.get_barrier_semaphore()
    for device in groups:
        pl.semaphore_signal(barrier, inc=1, device_id=device, device_id_type=MESH)
    pl.semaphore_wait(barrier, len(groups))


def remote(src, dst, send_sem, recv_sem, device):
    return pltpu.make_async_remote_copy(
        src_ref=src,
        dst_ref=dst,
        send_sem=send_sem,
        recv_sem=recv_sem,
        device_id=device,
        device_id_type=MESH,
    )


def others(axis, n):
    me = lax.axis_index(axis)
    return [lax.rem(me + d, n) for d in range(1, n)]


def exchange(n, buf, send_sem, recv_sem):
    me = lax.axis_index("batch")
    peers = others("batch", n)
    for peer in peers:
        remote(buf.at[me], buf.at[me], send_sem.at[peer], recv_sem.at[me], {"batch": peer}).start()
    for peer in peers:
        remote(
            buf.at[peer], buf.at[peer], send_sem.at[peer], recv_sem.at[peer], {"batch": peer}
        ).wait()
    total = buf[0]
    for k in range(1, n):
        total = total + buf[k]
    return total


def early_kernel(n_chan, n_batch, x_ref, w_ref, x_out, raw_out, sum_out, held, buf,
                 up_send, up_recv, down_send, down_recv, sum_send, sum_recv):
    z = lax.axis_index("chan")
    me = lax.axis_index("batch")
    rows = x_ref.shape[0]
    meet([{"chan": p} for p in others("chan", n_chan)]
         + [{"batch": p} for p in others("batch", n_batch)])
    held[z] = x_ref[...]

    def up(block):
        return remote(held.at[block], held.at[block], up_send.at[block], up_recv.at[block],
                      {"chan": lax.rem(z + 1, n_chan)})

    def down(block):
        return remote(held.at[block], held.at[block], down_send.at[block], down_recv.at[block],
                      {"chan": lax.rem(z + n_chan - 1, n_chan)})

    @pl.when(z < n_chan - 1)
    def _():
        up(z).start()

    @pl.when(z > 0)
    def _():
        down(z).start()

    def multiply(block):
        at = pl.ds(pl.multiple_of(block * rows, rows), rows)
        width = w_ref.shape[1]
        step = min(width, 512)

        @pl.loop(0, width // step)
        def _(i):
            cols = pl.ds(pl.multiple_of(i * step, step), step)
            raw = jnp.dot(
                held[block], w_ref[:, cols], preferred_element_type=jnp.float32
            ).astype(jnp.bfloat16)
            raw_out[at, cols] = raw
            raw = raw.astype(jnp.float32)
            buf[me, 0:1, cols] += jnp.sum(raw, 0, keepdims=True)
            buf[me, 1:2, cols] += jnp.sum(raw * raw, 0, keepdims=True)

    buf[me] = jnp.zeros(buf.shape[1:], buf.dtype)
    multiply(z)
    for i in range(1, n_chan):
        below, above = z - i, z + i

        @pl.when(below >= 0)
        def _():
            up(below).wait_recv()

            @pl.when(z < n_chan - 1)
            def _():
                up(below).start()

        @pl.when(above < n_chan)
        def _():
            down(above).wait_recv()

            @pl.when(z > 0)
            def _():
                down(above).start()

        @pl.when(below >= 0)
        def _():
            multiply(below)

        @pl.when(above < n_chan)
        def _():
            multiply(above)

    sum_out[...] = exchange(n_batch, buf, sum_send, sum_recv)
    x_out[...] = held[...].reshape(x_out.shape)
    for block in range(n_chan):
        @pl.when(jnp.logical_and(block <= z, z < n_chan - 1))
        def _():
            up(block).wait_send()

        @pl.when(jnp.logical_and(block >= z, z > 0))
        def _():
            down(block).wait_send()


def early_forward(x, w, collective_id):
    n_chan, n_batch = lax.axis_size("chan"), lax.axis_size("batch")
    rows, width_in = x.shape
    width = w.shape[1]
    return pl.pallas_call(
        functools.partial(early_kernel, n_chan, n_batch),
        out_shape=(
            jax.ShapeDtypeStruct((n_chan * rows, width_in), x.dtype),
            jax.ShapeDtypeStruct((n_chan * rows, width), x.dtype),
            jax.ShapeDtypeStruct((8, width), jnp.float32),
        ),
        in_specs=[pl.BlockSpec(memory_space=pltpu.VMEM)] * 2,
        out_specs=[pl.BlockSpec(memory_space=pltpu.VMEM)] * 3,
        scratch_shapes=[
            pltpu.VMEM((n_chan, rows, width_in), x.dtype),
            pltpu.VMEM((n_batch, 8, width), jnp.float32),
        ]
        + [pltpu.SemaphoreType.DMA((n_chan,))] * 4
        + [pltpu.SemaphoreType.DMA((n_batch,))] * 2,
        compiler_params=pltpu.CompilerParams(
            collective_id=collective_id, has_side_effects=True, vmem_limit_bytes=56 * 2**20
        ),
        name="early_forward",
    )(x, w)


CHUNKS = 4


def backward_kernel(n_sec, n_chan, n_batch, act_ref, gh_ref, vec_ref, w_hbm, raw_hbm, x_hbm,
                    late_ref, early_ref, w_ref, raw_ref, x_ref, give, held, gact, buf,
                    fa, fb, sa, sb, part, pair, mine, low, high, last,
                    load_sem, put_sem, p1s, p1r, fas, far, fbs, fbr, sas, sar, sbs, sbr,
                    cas, car, cbs, cbr, p5s, p5r, sum_send, sum_recv,
                    pair_send, pair_recv, low_send, low_recv, high_send, high_recv,
                    last_send, last_recv):
    s, z, b = lax.axis_index("section"), lax.axis_index("chan"), lax.axis_index("batch")
    n_y = n_batch // 2
    y, core = b // 2, lax.rem(b, 2)
    sibling = {"batch": y * 2 + 1 - core}
    plane = [
        (lax.rem(s + i, n_sec), lax.rem(y + j, n_y))
        for i in range(n_sec) for j in range(n_y) if i + j > 0
    ]
    inner = [
        (lax.rem(s + i, n_sec), lax.rem(y + j, n_y))
        for i in range(1, n_sec) for j in range(1, n_y)
    ]
    loads = [
        pltpu.make_async_copy(w_hbm, w_ref, load_sem.at[0]),
        pltpu.make_async_copy(raw_hbm, raw_ref, load_sem.at[1]),
        pltpu.make_async_copy(x_hbm, x_ref, load_sem.at[2]),
    ]
    for load in loads:
        load.start()
    meet([{"batch": p} for p in others("batch", n_batch)]
         + [{"chan": p} for p in others("chan", n_chan)]
         + [{"section": p} for p in others("section", n_sec)]
         + [{"section": p, "batch": q * 2 + core} for p, q in inner])

    f32, bf16 = jnp.float32, jnp.bfloat16
    images, mid = act_ref.shape
    wide = gh_ref.shape[1]
    chunk = mid // CHUNKS
    half, tall = chunk // 2, chunk // 4
    step = min(wide, 512)

    def dev_sec(p):
        return {"section": p}

    def dev_y(q):
        return {"batch": q * 2 + core}

    kinds = [
        (n_sec, s, dev_sec, n_y, y, dev_y, fa, sa, fas, far, sas, sar, cas, car),
        (n_y, y, dev_y, n_sec, s, dev_sec, fb, sb, fbs, fbr, sbs, sbr, cbs, cbr),
    ]

    def span_of(k, t, p):
        sub = tall // kinds[t][0]
        return pl.ds(pl.multiple_of(k * chunk + core * half + t * tall + p * sub, sub), sub)

    def to_pair(k):
        return remote(give.at[k], held.at[k], p1s.at[k], p1r.at[k], sibling)

    def first(k, t, p, slot):
        n1, me, dev, _, _, _, buf1, _, ss, rs = kinds[t][:10]
        sub = tall // n1
        return remote(held.at[k, pl.ds(pl.multiple_of(t * tall + p * sub, sub), sub)],
                      buf1.at[k, slot], ss.at[k * n1 + p], rs.at[k * n1 + slot], dev(p))

    def second(k, t, q, slot):
        _, _, _, n2, me, dev, _, buf2, _, _, ss, rs = kinds[t][:12]
        return remote(buf2.at[k, me], buf2.at[k, slot], ss.at[k * n2 + q], rs.at[k * n2 + slot], dev(q))

    def third(k, t, p, slot):
        n1, me, dev, _, _, _, buf1 = kinds[t][:7]
        ss, rs = kinds[t][12:]
        return remote(buf1.at[k, me], late_ref.at[span_of(k, t, slot)], ss.at[k * n1 + p],
                      rs.at[k * n1 + slot], dev(p))

    def keep(k, t):
        me, buf1 = kinds[t][1], kinds[t][6]
        return pltpu.make_async_copy(buf1.at[k, me], late_ref.at[span_of(k, t, me)],
                                     put_sem.at[k * 2 + t])

    def share(k, which):
        rows = pl.ds(pl.multiple_of(k * chunk + which * half, half), half)
        return remote(late_ref.at[rows], late_ref.at[rows], p5s.at[k], p5r.at[k], sibling)

    def peers_of(n, me):
        return [lax.rem(me + d, n) for d in range(1, n)]

    def product(k):
        def run(which, dst, add):
            start = pl.multiple_of(k * chunk + which * half, half)
            lhs = act_ref[:, pl.ds(start, half)].T

            @pl.loop(0, wide // step)
            def _(i):
                cols = pl.ds(pl.multiple_of(i * step, step), step)
                block = jnp.dot(lhs, gh_ref[:, cols], preferred_element_type=f32)
                if add:
                    block = block + dst[k, :, cols].astype(f32)
                dst[k, :, cols] = block.astype(bf16)

        run(1 - core, give, False)
        to_pair(k).start()
        to_own = k - 1
        return run, to_own

    def own_product(k, run):
        to_pair(k).wait_recv()
        run(core, held, True)
        for t in range(2):
            n1, me = kinds[t][:2]
            for p in peers_of(n1, me):
                first(k, t, p, me).start()

    waiting = None
    for k in range(CHUNKS):
        run, _ = product(k)
        if waiting is not None:
            own_product(k - 1, waiting)
        waiting = run
    own_product(CHUNKS - 1, waiting)

    def scatter_done(k):
        for t in range(2):
            n1, me, _, n2, me2, _, buf1, buf2 = kinds[t][:8]
            sub = tall // n1
            total = held[k, pl.ds(pl.multiple_of(t * tall + me * sub, sub), sub)].astype(f32)
            for p in peers_of(n1, me):
                first(k, t, p, p).wait_recv()
                total = total + buf1[k, p].astype(f32)
            buf2[k, me2] = total.astype(bf16)
            for q in peers_of(n2, me2):
                second(k, t, q, me2).start()

    def sum_done(k):
        for t in range(2):
            n1, me, _, n2, me2, _, buf1, buf2 = kinds[t][:8]
            for q in peers_of(n2, me2):
                second(k, t, q, q).wait_recv()
            total = buf2[k, 0].astype(f32)
            for j in range(1, n2):
                total = total + buf2[k, j].astype(f32)
            buf1[k, me] = total.astype(bf16)
            for p in peers_of(n1, me):
                third(k, t, p, me).start()
            keep(k, t).start()

    def gather_done(k):
        for t in range(2):
            n1, me = kinds[t][:2]
            for p in peers_of(n1, me):
                third(k, t, p, p).wait_recv()
            keep(k, t).wait()
        share(k, core).start()

    for load in loads:
        load.wait()
    buf[b] = jnp.zeros(buf.shape[1:], f32)
    lane = 256
    tile = 512

    def sig(v):
        return 1.0 / (1.0 + jnp.exp(-v))

    def chain(i):
        cols = pl.ds(pl.multiple_of(i * lane, lane), lane)
        mean, rstd = vec_ref[0:1, cols], vec_ref[1:2, cols]
        gain, bias = vec_ref[2:3, cols], vec_ref[3:4, cols]

        @pl.loop(0, images // tile)
        def _(j):
            rows = pl.ds(pl.multiple_of(j * tile, tile), tile)
            grad = lax.dot_general(
                gh_ref[rows, :], w_ref[cols, :], (((1,), (1,)), ((), ())),
                preferred_element_type=f32,
            )
            normed = (raw_ref[rows, cols].astype(f32) - mean) * rstd
            pre = normed * gain + bias
            gate = sig(pre)
            grad = grad * (gate * (1.0 + pre * (1.0 - gate)))
            buf[b, 0:1, cols] += jnp.sum(grad, 0, keepdims=True)
            buf[b, 1:2, cols] += jnp.sum(grad * normed, 0, keepdims=True)
            gact[rows, cols] = grad.astype(bf16)

    tiles = mid // lane
    for k in range(CHUNKS):
        @pl.loop(k * tiles // CHUNKS, (k + 1) * tiles // CHUNKS)
        def _(i):
            chain(i)

        scatter_done(k)

    sums = exchange(n_batch, buf, sum_send, sum_recv)
    count = images * n_batch
    buf[b] = sums / count

    @pl.loop(0, mid // lane)
    def _(i):
        cols = pl.ds(pl.multiple_of(i * lane, lane), lane)
        mean, rstd, gain = vec_ref[0:1, cols], vec_ref[1:2, cols], vec_ref[2:3, cols]
        one, two = buf[b, 0:1, cols], buf[b, 1:2, cols]

        @pl.loop(0, images // lane)
        def _(j):
            rows = pl.ds(pl.multiple_of(j * lane, lane), lane)
            normed = (raw_ref[rows, cols].astype(f32) - mean) * rstd
            grad = gact[rows, cols].astype(f32)
            gact[rows, cols] = (gain * rstd * (grad - one - normed * two)).astype(bf16)

    rows, width = early_ref.shape
    span = rows * n_batch
    step_e = min(width, 512)
    order = []
    for i in range(n_chan // 2):
        order += [i, n_chan - 1 - i]

    def early_part(d):
        lhs = jnp.concatenate(
            [x_ref[:, (k * n_chan + d) * span:(k * n_chan + d + 1) * span] for k in range(n_sec)], 1
        ).T

        @pl.loop(0, width // step_e)
        def _(i):
            cols = pl.ds(pl.multiple_of(i * step_e, step_e), step_e)
            block = jnp.dot(lhs, gact[:, cols], preferred_element_type=f32)
            part[d, :, :, :, :, cols] = block.reshape(n_sec, n_y, 2, rows, step_e).astype(bf16)

        pair_copy(d).start()

    def pair_copy(d):
        return remote(part.at[d, :, :, 1 - core], pair.at[d], pair_send.at[d], pair_recv.at[d], sibling)

    def from_pair(d):
        pair_copy(d).wait_recv()
        mine[d] = (part[d, :, :, core].astype(f32) + pair[d].astype(f32)).astype(bf16)

    def lower(d):
        return remote(mine.at[d], low.at[d], low_send.at[d], low_recv.at[d],
                      {"chan": lax.rem(z + n_chan - 1, n_chan)})

    def upper(d):
        return remote(mine.at[d], high.at[d], high_send.at[d], high_recv.at[d],
                      {"chan": lax.rem(z + 1, n_chan)})

    def add(d, arrived):
        mine[d] = (mine[d].astype(f32) + arrived[d].astype(f32)).astype(bf16)

    def ready(d):
        from_pair(d)

        @pl.when(jnp.logical_and(z == n_chan - 1, d < z))
        def _():
            lower(d).start()

        @pl.when(jnp.logical_and(z == 0, d > z))
        def _():
            upper(d).start()

    for n, d in enumerate(order):
        early_part(d)
        if n > 0:
            ready(order[n - 1])
    ready(order[-1])
    sum_done(0)
    sum_done(1)

    later = [lambda k=k: sum_done(k) for k in range(2, CHUNKS)]
    later += [lambda k=k: gather_done(k) for k in range(CHUNKS)]
    for i in range(n_chan):
        d, e = i, n_chan - 1 - i

        @pl.when(jnp.logical_and(z < n_chan - 1, d <= z))
        def _():
            lower(d).wait_recv()
            add(d, low)

            @pl.when(d < z)
            def _():
                lower(d).start()

        @pl.when(jnp.logical_and(z > 0, e >= z))
        def _():
            upper(e).wait_recv()
            add(e, high)

            @pl.when(e > z)
            def _():
                upper(e).start()

        if i < 2:
            for act_now in later[:2]:
                act_now()
            later = later[2:]

    slot = s * n_y + y
    for p, q in plane:
        remote(mine.at[z, p, q], last.at[slot], last_send.at[p * n_y + q], last_recv.at[slot],
               {"section": p, "batch": q * 2 + core}).start()
    for act_now in later:
        act_now()
    total = mine[z, s, y].astype(f32)
    for p, q in plane:
        there = p * n_y + q
        remote(mine.at[z, p, q], last.at[there], last_send.at[there], last_recv.at[there],
               {"section": p, "batch": q * 2 + core}).wait()
        total = total + last[there].astype(f32)
    early_ref[...] = total
    for d in range(n_chan):
        pair_copy(d).wait_send()

        @pl.when(d < z)
        def _():
            lower(d).wait_send()

        @pl.when(d > z)
        def _():
            upper(d).wait_send()

    for k in range(CHUNKS):
        share(k, 1 - core).wait_recv()
        share(k, core).wait_send()
        to_pair(k).wait_send()
        for t in range(2):
            n1, me, _, n2, me2 = kinds[t][:5]
            for p in peers_of(n1, me):
                first(k, t, p, me).wait_send()
                third(k, t, p, me).wait_send()
            for q in peers_of(n2, me2):
                second(k, t, q, me2).wait_send()


def backward(act, grad_h, vectors, w_late, raw, x, collective_id):
    n_sec, n_chan, n_batch = (lax.axis_size(a) for a in ("section", "chan", "batch"))
    n_y = n_batch // 2
    mid, wide = w_late.shape
    rows = x.shape[1] // (n_sec * n_chan * n_batch)
    quarter = (n_chan, n_sec, n_y, rows, mid)
    half, tall = mid // CHUNKS // 2, mid // CHUNKS // 4
    bf16 = jnp.bfloat16
    vmem, anywhere = pl.BlockSpec(memory_space=pltpu.VMEM), pl.BlockSpec(memory_space=pl.ANY)
    sems = [3, 2 * CHUNKS, CHUNKS, CHUNKS]
    sems += [CHUNKS * n for n in (n_sec, n_sec, n_y, n_y, n_y, n_y, n_sec, n_sec, n_sec, n_sec, n_y, n_y)]
    sems += [CHUNKS, CHUNKS, n_batch, n_batch] + [n_chan] * 6 + [n_sec * n_y] * 2
    return pl.pallas_call(
        functools.partial(backward_kernel, n_sec, n_chan, n_batch),
        out_shape=(
            jax.ShapeDtypeStruct((mid, wide), bf16),
            jax.ShapeDtypeStruct((rows, mid), jnp.float32),
        ),
        in_specs=[vmem, vmem, vmem, anywhere, anywhere, anywhere],
        out_specs=[anywhere, vmem],
        scratch_shapes=[
            pltpu.VMEM(w_late.shape, bf16),
            pltpu.VMEM(raw.shape, bf16),
            pltpu.VMEM(x.shape, bf16),
            pltpu.VMEM((CHUNKS, half, wide), bf16),
            pltpu.VMEM((CHUNKS, half, wide), bf16),
            pltpu.VMEM(raw.shape, bf16),
            pltpu.VMEM((n_batch, 8, mid), jnp.float32),
            pltpu.VMEM((CHUNKS, n_sec, tall // n_sec, wide), bf16),
            pltpu.VMEM((CHUNKS, n_y, tall // n_y, wide), bf16),
            pltpu.VMEM((CHUNKS, n_y, tall // n_sec, wide), bf16),
            pltpu.VMEM((CHUNKS, n_sec, tall // n_y, wide), bf16),
            pltpu.VMEM((n_chan, n_sec, n_y, 2, rows, mid), bf16),
        ]
        + [pltpu.VMEM(quarter, bf16)] * 4
        + [pltpu.VMEM((n_sec * n_y, rows, mid), bf16)]
        + [pltpu.SemaphoreType.DMA((n,)) for n in sems],
        compiler_params=pltpu.CompilerParams(
            collective_id=collective_id, has_side_effects=True, vmem_limit_bytes=63 * 2**20
        ),
        name="backward",
    )(act, grad_h, vectors, w_late, raw, x)


def body(images, w_early, gain_early, bias_early, w_late, gain_late, bias_late, cotangent):
    width_in = images.shape[-1]
    width_mid = w_early.shape[1]
    width_out = w_late.shape[1]
    batch_count = lax.axis_size("batch")
    own = images.reshape(-1, width_in)
    flat_in, raw, sums_e = early_forward(own, w_early, 0)
    total_rows = flat_in.shape[0] * batch_count

    raw_f = raw.astype(jnp.float32)
    sum_one, sum_two = sums_e[0], sums_e[1]
    mean_e = sum_one / total_rows
    rstd_e = lax.rsqrt(sum_two / total_rows - mean_e * mean_e + 1e-05)
    normed_e = (raw_f - mean_e) * rstd_e
    pre_e = normed_e * gain_early + bias_early
    act = smooth_gate(pre_e).astype(jnp.bfloat16)

    late = jnp.dot(act, w_late, preferred_element_type=jnp.float32)
    late_one, late_two = batch_sums(jnp.sum(late, 0), jnp.sum(late * late, 0), 1)
    mean_l = late_one / total_rows
    rstd_l = lax.rsqrt(late_two / total_rows - mean_l * mean_l + 1e-05)
    normed_l = (late - mean_l) * rstd_l
    pre_l = normed_l * gain_late + bias_late
    late_out = smooth_gate(pre_l).astype(jnp.bfloat16).reshape(cotangent.shape)
    grad_y = cotangent.reshape(-1, width_out).astype(jnp.float32) * smooth_slope(pre_l)
    back_one, back_two = batch_sums(jnp.sum(grad_y, 0), jnp.sum(grad_y * normed_l, 0), 2)
    grad_h = (
        gain_late * rstd_l * (grad_y - back_one / total_rows - normed_l * (back_two / total_rows))
    ).astype(jnp.bfloat16)

    vectors = jnp.pad(jnp.stack([mean_e, rstd_e, gain_early, bias_early]), ((0, 4), (0, 0)))
    grad_late, grad_early = backward(act, grad_h, vectors, w_late, raw, flat_in, 4)
    grad_late = grad_late.astype(jnp.float32)
    return (late_out, grad_late, grad_early)


def solution(mesh):
    return jax.shard_map(
        body,
        mesh=mesh,
        in_specs=(
            P("section", "batch", "chan", None, None),
            P(),
            P(),
            P(),
            P(None, "chan"),
            P("chan"),
            P("chan"),
            P("section", "batch", None, "chan"),
        ),
        out_specs=(
            P("section", "batch", None, "chan"),
            P(None, "chan"),
            P(("section", "chan", "batch"), None),
        ),
        check_vma=False,
    )
```

```python
import functools

import jax
import jax.numpy as jnp
from jax import lax
from jax.experimental import pallas as pl
from jax.experimental.pallas import tpu as pltpu
from jax.sharding import PartitionSpec as P

MESH = pl.DeviceIdType.MESH


def meet(groups):
    barrier = pltpu.get_barrier_semaphore()
    for device in groups:
        pl.semaphore_signal(barrier, inc=1, device_id=device, device_id_type=MESH)
    pl.semaphore_wait(barrier, len(groups))


def remote(src, dst, send_sem, recv_sem, device):
    return pltpu.make_async_remote_copy(
        src_ref=src,
        dst_ref=dst,
        send_sem=send_sem,
        recv_sem=recv_sem,
        device_id=device,
        device_id_type=MESH,
    )


def others(axis, n):
    me = lax.axis_index(axis)
    return [lax.rem(me + d, n) for d in range(1, n)]


def exchange(n, buf, send_sem, recv_sem):
    me = lax.axis_index("batch")
    peers = others("batch", n)
    for peer in peers:
        remote(buf.at[me], buf.at[me], send_sem.at[peer], recv_sem.at[me], {"batch": peer}).start()
    for peer in peers:
        remote(
            buf.at[peer], buf.at[peer], send_sem.at[peer], recv_sem.at[peer], {"batch": peer}
        ).wait()
    total = buf[0]
    for k in range(1, n):
        total = total + buf[k]
    return total


def early_kernel(n_chan, n_batch, x_ref, w_ref, x_out, raw_out, sum_out, held, buf,
                 up_send, up_recv, down_send, down_recv, sum_send, sum_recv):
    z = lax.axis_index("chan")
    me = lax.axis_index("batch")
    rows = x_ref.shape[0]
    meet([{"chan": p} for p in others("chan", n_chan)]
         + [{"batch": p} for p in others("batch", n_batch)])
    held[z] = x_ref[...]

    def up(block):
        return remote(held.at[block], held.at[block], up_send.at[block], up_recv.at[block],
                      {"chan": lax.rem(z + 1, n_chan)})

    def down(block):
        return remote(held.at[block], held.at[block], down_send.at[block], down_recv.at[block],
                      {"chan": lax.rem(z + n_chan - 1, n_chan)})

    @pl.when(z < n_chan - 1)
    def _():
        up(z).start()

    @pl.when(z > 0)
    def _():
        down(z).start()

    def multiply(block):
        at = pl.ds(pl.multiple_of(block * rows, rows), rows)
        width = w_ref.shape[1]
        step = min(width, 512)

        @pl.loop(0, width // step)
        def _(i):
            cols = pl.ds(pl.multiple_of(i * step, step), step)
            raw = jnp.dot(
                held[block], w_ref[:, cols], preferred_element_type=jnp.float32
            ).astype(jnp.bfloat16)
            raw_out[at, cols] = raw
            raw = raw.astype(jnp.float32)
            buf[me, 0:1, cols] += jnp.sum(raw, 0, keepdims=True)
            buf[me, 1:2, cols] += jnp.sum(raw * raw, 0, keepdims=True)

    buf[me] = jnp.zeros(buf.shape[1:], buf.dtype)
    multiply(z)
    for i in range(1, n_chan):
        below, above = z - i, z + i

        @pl.when(below >= 0)
        def _():
            up(below).wait_recv()

            @pl.when(z < n_chan - 1)
            def _():
                up(below).start()

        @pl.when(above < n_chan)
        def _():
            down(above).wait_recv()

            @pl.when(z > 0)
            def _():
                down(above).start()

        @pl.when(below >= 0)
        def _():
            multiply(below)

        @pl.when(above < n_chan)
        def _():
            multiply(above)

    sum_out[...] = exchange(n_batch, buf, sum_send, sum_recv)
    x_out[...] = held[...].reshape(x_out.shape)
    for block in range(n_chan):
        @pl.when(jnp.logical_and(block <= z, z < n_chan - 1))
        def _():
            up(block).wait_send()

        @pl.when(jnp.logical_and(block >= z, z > 0))
        def _():
            down(block).wait_send()


def early_forward(x, w, collective_id):
    n_chan, n_batch = lax.axis_size("chan"), lax.axis_size("batch")
    rows, width_in = x.shape
    width = w.shape[1]
    return pl.pallas_call(
        functools.partial(early_kernel, n_chan, n_batch),
        out_shape=(
            jax.ShapeDtypeStruct((n_chan * rows, width_in), x.dtype),
            jax.ShapeDtypeStruct((n_chan * rows, width), x.dtype),
            jax.ShapeDtypeStruct((8, width), jnp.float32),
        ),
        in_specs=[pl.BlockSpec(memory_space=pltpu.VMEM)] * 2,
        out_specs=[pl.BlockSpec(memory_space=pltpu.VMEM)] * 3,
        scratch_shapes=[
            pltpu.VMEM((n_chan, rows, width_in), x.dtype),
            pltpu.VMEM((n_batch, 8, width), jnp.float32),
        ]
        + [pltpu.SemaphoreType.DMA((n_chan,))] * 4
        + [pltpu.SemaphoreType.DMA((n_batch,))] * 2,
        compiler_params=pltpu.CompilerParams(
            collective_id=collective_id, has_side_effects=True, vmem_limit_bytes=56 * 2**20
        ),
        name="early_forward",
    )(x, w)


CHUNKS = 4
STRIP = 64


def half_gate(v):
    return 0.5 * jnp.tanh(0.5 * v) + 0.5


def fold(v):
    return jnp.sum(v.reshape(-1, 8, v.shape[1]), 0)


def late_kernel(n_batch, raw_ref, vec_ref, lvec_ref, w_ref, cot_hbm, act_ref, out_ref, gh_ref,
                cot_ref, hidden, grad_y, buf, back, cot_sem, sum_send, sum_recv, back_send, back_recv):
    b = lax.axis_index("batch")
    load = pltpu.make_async_copy(cot_hbm, cot_ref, cot_sem)
    load.start()
    meet([{"batch": p} for p in others("batch", n_batch)])
    f32, bf16 = jnp.float32, jnp.bfloat16
    rows, mid = raw_ref.shape
    wide = w_ref.shape[1]
    lane = 256
    buf[b] = jnp.zeros(buf.shape[1:], f32)

    @pl.loop(0, mid // lane)
    def _(i):
        cols = pl.ds(pl.multiple_of(i * lane, lane), lane)
        scale = vec_ref[1:2, cols] * vec_ref[2:3, cols]
        shift = vec_ref[3:4, cols] - vec_ref[0:1, cols] * scale

        def strip(r, carry):
            here = pl.ds(pl.multiple_of(r * STRIP, STRIP), STRIP)
            pre = raw_ref[here, cols].astype(f32) * scale + shift
            act_ref[here, cols] = (pre * half_gate(pre)).astype(bf16)
            return carry

        lax.fori_loop(0, rows // STRIP, strip, 0, unroll=2)

    tile = 512

    @pl.loop(0, wide // lane)
    def _(i):
        cols = pl.ds(pl.multiple_of(i * lane, lane), lane)

        @pl.loop(0, rows // tile)
        def _(j):
            here = pl.ds(pl.multiple_of(j * tile, tile), tile)
            block = jnp.dot(act_ref[here, :], w_ref[:, cols], preferred_element_type=f32)
            hidden[here, cols] = block
            buf[b, 0:1, cols] += jnp.sum(block, 0, keepdims=True)
            buf[b, 1:2, cols] += jnp.sum(block * block, 0, keepdims=True)

    sums = exchange(n_batch, buf, sum_send, sum_recv)
    count = rows * n_batch
    mean = sums[0:1] / count
    buf[b, 0:1] = mean
    buf[b, 1:2] = lax.rsqrt(sums[1:2] / count - mean * mean + 1e-05)
    load.wait()

    @pl.loop(0, wide // lane)
    def _(i):
        cols = pl.ds(pl.multiple_of(i * lane, lane), lane)
        mean, rstd = buf[b, 0:1, cols], buf[b, 1:2, cols]
        gain, bias = lvec_ref[0:1, cols], lvec_ref[1:2, cols]

        def strip(r, sums):
            here = pl.ds(pl.multiple_of(r * STRIP, STRIP), STRIP)
            normed = (hidden[here, cols] - mean) * rstd
            pre = normed * gain + bias
            gate = half_gate(pre)
            out_ref[here, cols] = (pre * gate).astype(bf16)
            grad = cot_ref[here, cols].astype(f32) * (gate * (1.0 + pre * (1.0 - gate)))
            hidden[here, cols] = normed
            grad_y[here, cols] = grad
            return sums[0] + fold(grad), sums[1] + fold(grad * normed)

        zero = jnp.zeros((8, lane), f32)
        one, two = lax.fori_loop(0, rows // STRIP, strip, (zero, zero), unroll=2)
        back[b, :, cols] = jnp.concatenate(
            [jnp.sum(one, 0, keepdims=True), jnp.sum(two, 0, keepdims=True), zero[:6]], 0
        )

    back[b] = exchange(n_batch, back, back_send, back_recv) / count

    @pl.loop(0, wide // lane)
    def _(i):
        cols = pl.ds(pl.multiple_of(i * lane, lane), lane)
        scale = buf[b, 1:2, cols] * lvec_ref[0:1, cols]
        one, two = back[b, 0:1, cols], back[b, 1:2, cols]

        def strip(r, carry):
            here = pl.ds(pl.multiple_of(r * STRIP, STRIP), STRIP)
            gh_ref[here, cols] = (
                scale * (grad_y[here, cols] - one - hidden[here, cols] * two)
            ).astype(bf16)
            return carry

        lax.fori_loop(0, rows // STRIP, strip, 0, unroll=2)


def late_layer(raw, vectors, late_vectors, w_late, cotangent, collective_id):
    n_batch = lax.axis_size("batch")
    rows = raw.shape[0]
    mid, wide = w_late.shape
    vmem, anywhere = pl.BlockSpec(memory_space=pltpu.VMEM), pl.BlockSpec(memory_space=pl.ANY)
    f32, bf16 = jnp.float32, jnp.bfloat16
    return pl.pallas_call(
        functools.partial(late_kernel, n_batch),
        out_shape=(
            jax.ShapeDtypeStruct((rows, mid), bf16),
            jax.ShapeDtypeStruct((rows, wide), bf16),
            jax.ShapeDtypeStruct((rows, wide), bf16),
        ),
        in_specs=[vmem] * 4 + [anywhere],
        out_specs=[vmem] * 3,
        scratch_shapes=[
            pltpu.VMEM((rows, wide), bf16),
            pltpu.VMEM((rows, wide), f32),
            pltpu.VMEM((rows, wide), f32),
            pltpu.VMEM((n_batch, 8, wide), f32),
            pltpu.VMEM((n_batch, 8, wide), f32),
            pltpu.SemaphoreType.DMA,
        ]
        + [pltpu.SemaphoreType.DMA((n_batch,))] * 4,
        compiler_params=pltpu.CompilerParams(
            collective_id=collective_id, has_side_effects=True, vmem_limit_bytes=62 * 2**20
        ),
        name="late_layer",
    )(raw, vectors, late_vectors, w_late, cotangent)


def backward_kernel(n_sec, n_chan, n_batch, act_ref, gh_ref, vec_ref, w_hbm, raw_hbm, x_hbm,
                    late_ref, early_ref, w_ref, raw_ref, x_ref, give, held, gact, buf,
                    fa, fb, sa, sb, part, pair, mine, low, high, last, square,
                    load_sem, put_sem, p1s, p1r, fas, far, fbs, fbr, sas, sar, sbs, sbr,
                    cas, car, cbs, cbr, p5s, p5r, sum_send, sum_recv,
                    pair_send, pair_recv, low_send, low_recv, high_send, high_recv,
                    last_send, last_recv):
    s, z, b = lax.axis_index("section"), lax.axis_index("chan"), lax.axis_index("batch")
    n_y = n_batch // 2
    y, core = b // 2, lax.rem(b, 2)
    sibling = {"batch": y * 2 + 1 - core}
    plane = [
        (lax.rem(s + i, n_sec), lax.rem(y + j, n_y))
        for i in range(n_sec) for j in range(n_y) if i + j > 0
    ]
    inner = [
        (lax.rem(s + i, n_sec), lax.rem(y + j, n_y))
        for i in range(1, n_sec) for j in range(1, n_y)
    ]
    loads = [
        pltpu.make_async_copy(w_hbm, w_ref, load_sem.at[0]),
        pltpu.make_async_copy(raw_hbm, raw_ref, load_sem.at[1]),
        pltpu.make_async_copy(x_hbm, x_ref, load_sem.at[2]),
    ]
    for load in loads:
        load.start()
    meet([{"batch": p} for p in others("batch", n_batch)]
         + [{"chan": p} for p in others("chan", n_chan)]
         + [{"section": p} for p in others("section", n_sec)]
         + [{"section": p, "batch": q * 2 + core} for p, q in inner])

    f32, bf16 = jnp.float32, jnp.bfloat16
    images, mid = act_ref.shape
    wide = gh_ref.shape[1]
    chunk = mid // CHUNKS
    half, tall = chunk // 2, chunk // 4
    step = min(wide, 512)

    def dev_sec(p):
        return {"section": p}

    def dev_y(q):
        return {"batch": q * 2 + core}

    kinds = [
        (n_sec, s, dev_sec, n_y, y, dev_y, fa, sa, fas, far, sas, sar, cas, car),
        (n_y, y, dev_y, n_sec, s, dev_sec, fb, sb, fbs, fbr, sbs, sbr, cbs, cbr),
    ]

    def span_of(k, t, p):
        sub = tall // kinds[t][0]
        return pl.ds(pl.multiple_of(k * chunk + core * half + t * tall + p * sub, sub), sub)

    def to_pair(k):
        return remote(give.at[k], held.at[k], p1s.at[k], p1r.at[k], sibling)

    def first(k, t, p, slot):
        n1, me, dev, _, _, _, buf1, _, ss, rs = kinds[t][:10]
        sub = tall // n1
        return remote(held.at[k, pl.ds(pl.multiple_of(t * tall + p * sub, sub), sub)],
                      buf1.at[k, slot], ss.at[k * n1 + p], rs.at[k * n1 + slot], dev(p))

    def second(k, t, q, slot):
        _, _, _, n2, me, dev, _, buf2, _, _, ss, rs = kinds[t][:12]
        return remote(buf2.at[k, me], buf2.at[k, slot], ss.at[k * n2 + q], rs.at[k * n2 + slot], dev(q))

    def third(k, t, p, slot):
        n1, me, dev, _, _, _, buf1 = kinds[t][:7]
        ss, rs = kinds[t][12:]
        return remote(buf1.at[k, me], late_ref.at[span_of(k, t, slot)], ss.at[k * n1 + p],
                      rs.at[k * n1 + slot], dev(p))

    def keep(k, t):
        me, buf1 = kinds[t][1], kinds[t][6]
        return pltpu.make_async_copy(buf1.at[k, me], late_ref.at[span_of(k, t, me)],
                                     put_sem.at[k * 2 + t])

    def share(k, which):
        rows = pl.ds(pl.multiple_of(k * chunk + which * half, half), half)
        return remote(late_ref.at[rows], late_ref.at[rows], p5s.at[k], p5r.at[k], sibling)

    def peers_of(n, me):
        return [lax.rem(me + d, n) for d in range(1, n)]

    def product(k):
        def run(which, dst, add):
            start = pl.multiple_of(k * chunk + which * half, half)
            lhs = act_ref[:, pl.ds(start, half)].T

            @pl.loop(0, wide // step)
            def _(i):
                cols = pl.ds(pl.multiple_of(i * step, step), step)
                block = jnp.dot(lhs, gh_ref[:, cols], preferred_element_type=f32)
                if add:
                    block = block + dst[k, :, cols].astype(f32)
                dst[k, :, cols] = block.astype(bf16)

        run(1 - core, give, False)
        to_pair(k).start()
        return run

    def own_product(k, run):
        to_pair(k).wait_recv()
        run(core, held, True)
        for t in range(2):
            n1, me = kinds[t][:2]
            for p in peers_of(n1, me):
                first(k, t, p, me).start()

    waiting = None
    for k in range(CHUNKS):
        run = product(k)
        if waiting is not None:
            own_product(k - 1, waiting)
        waiting = run
    own_product(CHUNKS - 1, waiting)

    def scatter_done(k):
        for t in range(2):
            n1, me, _, n2, me2, _, buf1, buf2 = kinds[t][:8]
            sub = tall // n1
            total = held[k, pl.ds(pl.multiple_of(t * tall + me * sub, sub), sub)].astype(f32)
            for p in peers_of(n1, me):
                first(k, t, p, p).wait_recv()
                total = total + buf1[k, p].astype(f32)
            buf2[k, me2] = total.astype(bf16)
            for q in peers_of(n2, me2):
                second(k, t, q, me2).start()

    def sum_done(k):
        for t in range(2):
            n1, me, _, n2, me2, _, buf1, buf2 = kinds[t][:8]
            for q in peers_of(n2, me2):
                second(k, t, q, q).wait_recv()
            total = buf2[k, 0].astype(f32)
            for j in range(1, n2):
                total = total + buf2[k, j].astype(f32)
            buf1[k, me] = total.astype(bf16)
            for p in peers_of(n1, me):
                third(k, t, p, me).start()
            keep(k, t).start()

    def gather_done(k):
        for t in range(2):
            n1, me = kinds[t][:2]
            for p in peers_of(n1, me):
                third(k, t, p, p).wait_recv()
            keep(k, t).wait()
        share(k, core).start()

    for load in loads:
        load.wait()
    buf[b] = jnp.zeros(buf.shape[1:], f32)
    lane = 256
    tile = 512

    def chain(i):
        cols = pl.ds(pl.multiple_of(i * lane, lane), lane)
        mean, rstd = vec_ref[0:1, cols], vec_ref[1:2, cols]
        gain, bias = vec_ref[2:3, cols], vec_ref[3:4, cols]

        @pl.loop(0, images // tile)
        def _(j):
            rows = pl.ds(pl.multiple_of(j * tile, tile), tile)
            square[...] = lax.dot_general(
                gh_ref[rows, :], w_ref[cols, :], (((1,), (1,)), ((), ())),
                preferred_element_type=f32,
            )

            def strip(r, sums):
                here = pl.ds(pl.multiple_of(j * tile + r * STRIP, STRIP), STRIP)
                normed = (raw_ref[here, cols].astype(f32) - mean) * rstd
                pre = normed * gain + bias
                gate = half_gate(pre)
                grad = square[pl.ds(pl.multiple_of(r * STRIP, STRIP), STRIP), :]
                grad = grad * (gate * (1.0 + pre * (1.0 - gate)))
                gact[here, cols] = grad.astype(bf16)
                return sums[0] + fold(grad), sums[1] + fold(grad * normed)

            zero = jnp.zeros((8, lane), f32)
            one, two = lax.fori_loop(0, tile // STRIP, strip, (zero, zero), unroll=2)
            buf[b, 0:1, cols] += jnp.sum(one, 0, keepdims=True)
            buf[b, 1:2, cols] += jnp.sum(two, 0, keepdims=True)

    tiles = mid // lane
    for k in range(CHUNKS):
        @pl.loop(k * tiles // CHUNKS, (k + 1) * tiles // CHUNKS)
        def _(i):
            chain(i)

        scatter_done(k)

    sums = exchange(n_batch, buf, sum_send, sum_recv)
    count = images * n_batch
    buf[b] = sums / count

    @pl.loop(0, mid // lane)
    def _(i):
        cols = pl.ds(pl.multiple_of(i * lane, lane), lane)
        mean, rstd, gain = vec_ref[0:1, cols], vec_ref[1:2, cols], vec_ref[2:3, cols]
        one, two = buf[b, 0:1, cols], buf[b, 1:2, cols]

        @pl.loop(0, images // STRIP)
        def _(j):
            rows = pl.ds(pl.multiple_of(j * STRIP, STRIP), STRIP)
            normed = (raw_ref[rows, cols].astype(f32) - mean) * rstd
            grad = gact[rows, cols].astype(f32)
            gact[rows, cols] = (gain * rstd * (grad - one - normed * two)).astype(bf16)

    rows, width = early_ref.shape
    span = rows * n_batch
    step_e = min(width, 512)
    order = []
    for i in range(n_chan // 2):
        order += [i, n_chan - 1 - i]

    def early_part(d):
        lhs = jnp.concatenate(
            [x_ref[:, (k * n_chan + d) * span:(k * n_chan + d + 1) * span] for k in range(n_sec)], 1
        ).T

        @pl.loop(0, width // step_e)
        def _(i):
            cols = pl.ds(pl.multiple_of(i * step_e, step_e), step_e)
            block = jnp.dot(lhs, gact[:, cols], preferred_element_type=f32)
            part[d, :, :, :, :, cols] = block.reshape(n_sec, n_y, 2, rows, step_e).astype(bf16)

        pair_copy(d).start()

    def pair_copy(d):
        return remote(part.at[d, :, :, 1 - core], pair.at[d], pair_send.at[d], pair_recv.at[d], sibling)

    def from_pair(d):
        pair_copy(d).wait_recv()
        mine[d] = (part[d, :, :, core].astype(f32) + pair[d].astype(f32)).astype(bf16)

    def lower(d):
        return remote(mine.at[d], low.at[d], low_send.at[d], low_recv.at[d],
                      {"chan": lax.rem(z + n_chan - 1, n_chan)})

    def upper(d):
        return remote(mine.at[d], high.at[d], high_send.at[d], high_recv.at[d],
                      {"chan": lax.rem(z + 1, n_chan)})

    def add(d, arrived):
        mine[d] = (mine[d].astype(f32) + arrived[d].astype(f32)).astype(bf16)

    def ready(d):
        from_pair(d)

        @pl.when(jnp.logical_and(z == n_chan - 1, d < z))
        def _():
            lower(d).start()

        @pl.when(jnp.logical_and(z == 0, d > z))
        def _():
            upper(d).start()

    for n, d in enumerate(order):
        early_part(d)
        if n > 0:
            ready(order[n - 1])
        if n == 0 or n == 2:
            sum_done(n // 2)
    ready(order[-1])

    later = [lambda k=k: sum_done(k) for k in range(2, CHUNKS)]
    later += [lambda k=k: gather_done(k) for k in range(CHUNKS)]
    for i in range(n_chan):
        d, e = i, n_chan - 1 - i

        @pl.when(jnp.logical_and(z < n_chan - 1, d <= z))
        def _():
            lower(d).wait_recv()
            add(d, low)

            @pl.when(d < z)
            def _():
                lower(d).start()

        @pl.when(jnp.logical_and(z > 0, e >= z))
        def _():
            upper(e).wait_recv()
            add(e, high)

            @pl.when(e > z)
            def _():
                upper(e).start()

        if i < 2:
            for act_now in later[:2]:
                act_now()
            later = later[2:]

    slot = s * n_y + y
    for p, q in plane:
        remote(mine.at[z, p, q], last.at[slot], last_send.at[p * n_y + q], last_recv.at[slot],
               {"section": p, "batch": q * 2 + core}).start()
    for act_now in later:
        act_now()
    total = mine[z, s, y].astype(f32)
    for p, q in plane:
        there = p * n_y + q
        remote(mine.at[z, p, q], last.at[there], last_send.at[there], last_recv.at[there],
               {"section": p, "batch": q * 2 + core}).wait()
        total = total + last[there].astype(f32)
    early_ref[...] = total
    for d in range(n_chan):
        pair_copy(d).wait_send()

        @pl.when(d < z)
        def _():
            lower(d).wait_send()

        @pl.when(d > z)
        def _():
            upper(d).wait_send()

    for k in range(CHUNKS):
        share(k, 1 - core).wait_recv()
        share(k, core).wait_send()
        to_pair(k).wait_send()
        for t in range(2):
            n1, me, _, n2, me2 = kinds[t][:5]
            for p in peers_of(n1, me):
                first(k, t, p, me).wait_send()
                third(k, t, p, me).wait_send()
            for q in peers_of(n2, me2):
                second(k, t, q, me2).wait_send()


def backward(act, grad_h, vectors, w_late, raw, x, collective_id):
    n_sec, n_chan, n_batch = (lax.axis_size(a) for a in ("section", "chan", "batch"))
    n_y = n_batch // 2
    mid, wide = w_late.shape
    rows = x.shape[1] // (n_sec * n_chan * n_batch)
    quarter = (n_chan, n_sec, n_y, rows, mid)
    half, tall = mid // CHUNKS // 2, mid // CHUNKS // 4
    bf16 = jnp.bfloat16
    vmem, anywhere = pl.BlockSpec(memory_space=pltpu.VMEM), pl.BlockSpec(memory_space=pl.ANY)
    sems = [3, 2 * CHUNKS, CHUNKS, CHUNKS]
    sems += [CHUNKS * n for n in (n_sec, n_sec, n_y, n_y, n_y, n_y, n_sec, n_sec, n_sec, n_sec, n_y, n_y)]
    sems += [CHUNKS, CHUNKS, n_batch, n_batch] + [n_chan] * 6 + [n_sec * n_y] * 2
    return pl.pallas_call(
        functools.partial(backward_kernel, n_sec, n_chan, n_batch),
        out_shape=(
            jax.ShapeDtypeStruct((mid, wide), bf16),
            jax.ShapeDtypeStruct((rows, mid), jnp.float32),
        ),
        in_specs=[vmem, vmem, vmem, anywhere, anywhere, anywhere],
        out_specs=[anywhere, vmem],
        scratch_shapes=[
            pltpu.VMEM(w_late.shape, bf16),
            pltpu.VMEM(raw.shape, bf16),
            pltpu.VMEM(x.shape, bf16),
            pltpu.VMEM((CHUNKS, half, wide), bf16),
            pltpu.VMEM((CHUNKS, half, wide), bf16),
            pltpu.VMEM(raw.shape, bf16),
            pltpu.VMEM((n_batch, 8, mid), jnp.float32),
            pltpu.VMEM((CHUNKS, n_sec, tall // n_sec, wide), bf16),
            pltpu.VMEM((CHUNKS, n_y, tall // n_y, wide), bf16),
            pltpu.VMEM((CHUNKS, n_y, tall // n_sec, wide), bf16),
            pltpu.VMEM((CHUNKS, n_sec, tall // n_y, wide), bf16),
            pltpu.VMEM((n_chan, n_sec, n_y, 2, rows, mid), bf16),
        ]
        + [pltpu.VMEM(quarter, bf16)] * 4
        + [pltpu.VMEM((n_sec * n_y, rows, mid), bf16), pltpu.VMEM((512, 256), jnp.float32)]
        + [pltpu.SemaphoreType.DMA((n,)) for n in sems],
        compiler_params=pltpu.CompilerParams(
            collective_id=collective_id, has_side_effects=True, vmem_limit_bytes=63 * 2**20
        ),
        name="backward",
    )(act, grad_h, vectors, w_late, raw, x)


def body(images, w_early, gain_early, bias_early, w_late, gain_late, bias_late, cotangent):
    width_in = images.shape[-1]
    width_out = w_late.shape[1]
    batch_count = lax.axis_size("batch")
    own = images.reshape(-1, width_in)
    flat_in, raw, sums_e = early_forward(own, w_early, 0)
    total_rows = flat_in.shape[0] * batch_count

    mean_e = sums_e[0] / total_rows
    rstd_e = lax.rsqrt(sums_e[1] / total_rows - mean_e * mean_e + 1e-05)
    vectors = jnp.pad(jnp.stack([mean_e, rstd_e, gain_early, bias_early]), ((0, 4), (0, 0)))
    late_vectors = jnp.pad(jnp.stack([gain_late, bias_late]), ((0, 6), (0, 0)))
    act, late_out, grad_h = late_layer(
        raw, vectors, late_vectors, w_late, cotangent.reshape(-1, width_out), 1
    )
    late_out = late_out.reshape(cotangent.shape)

    grad_late, grad_early = backward(act, grad_h, vectors, w_late, raw, flat_in, 4)
    grad_late = grad_late.astype(jnp.float32)
    return (late_out, grad_late, grad_early)


def solution(mesh):
    return jax.shard_map(
        body,
        mesh=mesh,
        in_specs=(
            P("section", "batch", "chan", None, None),
            P(),
            P(),
            P(),
            P(None, "chan"),
            P("chan"),
            P("chan"),
            P("section", "batch", None, "chan"),
        ),
        out_specs=(
            P("section", "batch", None, "chan"),
            P(None, "chan"),
            P(("section", "chan", "batch"), None),
        ),
        check_vma=False,
    )
```

```python
import functools

import jax
import jax.numpy as jnp
from jax import lax
from jax.experimental import pallas as pl
from jax.experimental.pallas import tpu as pltpu
from jax.sharding import PartitionSpec as P

MESH = pl.DeviceIdType.MESH


def meet(groups):
    barrier = pltpu.get_barrier_semaphore()
    for device in groups:
        pl.semaphore_signal(barrier, inc=1, device_id=device, device_id_type=MESH)
    pl.semaphore_wait(barrier, len(groups))


def remote(src, dst, send_sem, recv_sem, device):
    return pltpu.make_async_remote_copy(
        src_ref=src,
        dst_ref=dst,
        send_sem=send_sem,
        recv_sem=recv_sem,
        device_id=device,
        device_id_type=MESH,
    )


def others(axis, n):
    me = lax.axis_index(axis)
    return [lax.rem(me + d, n) for d in range(1, n)]


def exchange(n, buf, send_sem, recv_sem):
    me = lax.axis_index("batch")
    peers = others("batch", n)
    for peer in peers:
        remote(buf.at[me], buf.at[me], send_sem.at[peer], recv_sem.at[me], {"batch": peer}).start()
    for peer in peers:
        remote(
            buf.at[peer], buf.at[peer], send_sem.at[peer], recv_sem.at[peer], {"batch": peer}
        ).wait()
    total = buf[0]
    for k in range(1, n):
        total = total + buf[k]
    return total


def early_kernel(n_chan, n_batch, x_ref, w_ref, x_out, raw_out, sum_out, held, buf,
                 up_send, up_recv, down_send, down_recv, sum_send, sum_recv):
    z = lax.axis_index("chan")
    me = lax.axis_index("batch")
    rows = x_ref.shape[0]
    meet([{"chan": p} for p in others("chan", n_chan)]
         + [{"batch": p} for p in others("batch", n_batch)])
    held[z] = x_ref[...]

    def up(block):
        return remote(held.at[block], held.at[block], up_send.at[block], up_recv.at[block],
                      {"chan": lax.rem(z + 1, n_chan)})

    def down(block):
        return remote(held.at[block], held.at[block], down_send.at[block], down_recv.at[block],
                      {"chan": lax.rem(z + n_chan - 1, n_chan)})

    @pl.when(z < n_chan - 1)
    def _():
        up(z).start()

    @pl.when(z > 0)
    def _():
        down(z).start()

    def multiply(block):
        at = pl.ds(pl.multiple_of(block * rows, rows), rows)
        width = w_ref.shape[1]
        step = min(width, 512)

        @pl.loop(0, width // step)
        def _(i):
            cols = pl.ds(pl.multiple_of(i * step, step), step)
            raw = jnp.dot(
                held[block], w_ref[:, cols], preferred_element_type=jnp.float32
            ).astype(jnp.bfloat16)
            raw_out[at, cols] = raw
            raw = raw.astype(jnp.float32)
            buf[me, 0:1, cols] += jnp.sum(raw, 0, keepdims=True)
            buf[me, 1:2, cols] += jnp.sum(raw * raw, 0, keepdims=True)

    buf[me] = jnp.zeros(buf.shape[1:], buf.dtype)
    multiply(z)
    for i in range(1, n_chan):
        below, above = z - i, z + i

        @pl.when(below >= 0)
        def _():
            up(below).wait_recv()

            @pl.when(z < n_chan - 1)
            def _():
                up(below).start()

        @pl.when(above < n_chan)
        def _():
            down(above).wait_recv()

            @pl.when(z > 0)
            def _():
                down(above).start()

        @pl.when(below >= 0)
        def _():
            multiply(below)

        @pl.when(above < n_chan)
        def _():
            multiply(above)

    sum_out[...] = exchange(n_batch, buf, sum_send, sum_recv)
    x_out[...] = held[...].reshape(x_out.shape)
    for block in range(n_chan):
        @pl.when(jnp.logical_and(block <= z, z < n_chan - 1))
        def _():
            up(block).wait_send()

        @pl.when(jnp.logical_and(block >= z, z > 0))
        def _():
            down(block).wait_send()


def early_forward(x, w, collective_id):
    n_chan, n_batch = lax.axis_size("chan"), lax.axis_size("batch")
    rows, width_in = x.shape
    width = w.shape[1]
    return pl.pallas_call(
        functools.partial(early_kernel, n_chan, n_batch),
        out_shape=(
            jax.ShapeDtypeStruct((n_chan * rows, width_in), x.dtype),
            jax.ShapeDtypeStruct((n_chan * rows, width), x.dtype),
            jax.ShapeDtypeStruct((8, width), jnp.float32),
        ),
        in_specs=[pl.BlockSpec(memory_space=pltpu.VMEM)] * 2,
        out_specs=[pl.BlockSpec(memory_space=pltpu.VMEM)] * 3,
        scratch_shapes=[
            pltpu.VMEM((n_chan, rows, width_in), x.dtype),
            pltpu.VMEM((n_batch, 8, width), jnp.float32),
        ]
        + [pltpu.SemaphoreType.DMA((n_chan,))] * 4
        + [pltpu.SemaphoreType.DMA((n_batch,))] * 2,
        compiler_params=pltpu.CompilerParams(
            collective_id=collective_id, has_side_effects=True, vmem_limit_bytes=56 * 2**20
        ),
        name="early_forward",
    )(x, w)


CHUNKS = 4
STRIP = 64


def half_gate(v):
    return 0.5 * jnp.tanh(0.5 * v) + 0.5


def fold(v):
    return jnp.sum(v.reshape(-1, 8, v.shape[1]), 0)


def late_kernel(n_batch, raw_ref, vec_ref, lvec_ref, w_ref, cot_hbm, act_ref, out_ref, gh_ref,
                cot_ref, hidden, grad_y, buf, back, cot_sem, sum_send, sum_recv, back_send, back_recv):
    b = lax.axis_index("batch")
    load = pltpu.make_async_copy(cot_hbm, cot_ref, cot_sem)
    load.start()
    meet([{"batch": p} for p in others("batch", n_batch)])
    f32, bf16 = jnp.float32, jnp.bfloat16
    rows, mid = raw_ref.shape
    wide = w_ref.shape[1]
    lane = 256
    buf[b] = jnp.zeros(buf.shape[1:], f32)

    @pl.loop(0, mid // lane)
    def _(i):
        cols = pl.ds(pl.multiple_of(i * lane, lane), lane)
        scale = vec_ref[1:2, cols] * vec_ref[2:3, cols]
        shift = vec_ref[3:4, cols] - vec_ref[0:1, cols] * scale

        def strip(r, carry):
            here = pl.ds(pl.multiple_of(r * STRIP, STRIP), STRIP)
            pre = raw_ref[here, cols].astype(f32) * scale + shift
            act_ref[here, cols] = (pre * half_gate(pre)).astype(bf16)
            return carry

        lax.fori_loop(0, rows // STRIP, strip, 0, unroll=2)

    tile = 512

    @pl.loop(0, wide // lane)
    def _(i):
        cols = pl.ds(pl.multiple_of(i * lane, lane), lane)

        @pl.loop(0, rows // tile)
        def _(j):
            here = pl.ds(pl.multiple_of(j * tile, tile), tile)
            block = jnp.dot(act_ref[here, :], w_ref[:, cols], preferred_element_type=f32)
            hidden[here, cols] = block
            buf[b, 0:1, cols] += jnp.sum(block, 0, keepdims=True)
            buf[b, 1:2, cols] += jnp.sum(block * block, 0, keepdims=True)

    sums = exchange(n_batch, buf, sum_send, sum_recv)
    count = rows * n_batch
    mean = sums[0:1] / count
    buf[b, 0:1] = mean
    buf[b, 1:2] = lax.rsqrt(sums[1:2] / count - mean * mean + 1e-05)
    load.wait()

    @pl.loop(0, wide // lane)
    def _(i):
        cols = pl.ds(pl.multiple_of(i * lane, lane), lane)
        mean, rstd = buf[b, 0:1, cols], buf[b, 1:2, cols]
        gain, bias = lvec_ref[0:1, cols], lvec_ref[1:2, cols]

        def strip(r, sums):
            here = pl.ds(pl.multiple_of(r * STRIP, STRIP), STRIP)
            normed = (hidden[here, cols] - mean) * rstd
            pre = normed * gain + bias
            gate = half_gate(pre)
            out_ref[here, cols] = (pre * gate).astype(bf16)
            grad = cot_ref[here, cols].astype(f32) * (gate * (1.0 + pre * (1.0 - gate)))
            hidden[here, cols] = normed
            grad_y[here, cols] = grad
            return sums[0] + fold(grad), sums[1] + fold(grad * normed)

        zero = jnp.zeros((8, lane), f32)
        one, two = lax.fori_loop(0, rows // STRIP, strip, (zero, zero), unroll=2)
        back[b, :, cols] = jnp.concatenate(
            [jnp.sum(one, 0, keepdims=True), jnp.sum(two, 0, keepdims=True), zero[:6]], 0
        )

    back[b] = exchange(n_batch, back, back_send, back_recv) / count

    @pl.loop(0, wide // lane)
    def _(i):
        cols = pl.ds(pl.multiple_of(i * lane, lane), lane)
        scale = buf[b, 1:2, cols] * lvec_ref[0:1, cols]
        one, two = back[b, 0:1, cols], back[b, 1:2, cols]

        def strip(r, carry):
            here = pl.ds(pl.multiple_of(r * STRIP, STRIP), STRIP)
            gh_ref[here, cols] = (
                scale * (grad_y[here, cols] - one - hidden[here, cols] * two)
            ).astype(bf16)
            return carry

        lax.fori_loop(0, rows // STRIP, strip, 0, unroll=2)


def late_layer(raw, vectors, late_vectors, w_late, cotangent, collective_id):
    n_batch = lax.axis_size("batch")
    rows = raw.shape[0]
    mid, wide = w_late.shape
    vmem, anywhere = pl.BlockSpec(memory_space=pltpu.VMEM), pl.BlockSpec(memory_space=pl.ANY)
    f32, bf16 = jnp.float32, jnp.bfloat16
    return pl.pallas_call(
        functools.partial(late_kernel, n_batch),
        out_shape=(
            jax.ShapeDtypeStruct((rows, mid), bf16),
            jax.ShapeDtypeStruct((rows, wide), bf16),
            jax.ShapeDtypeStruct((rows, wide), bf16),
        ),
        in_specs=[vmem] * 4 + [anywhere],
        out_specs=[vmem] * 3,
        scratch_shapes=[
            pltpu.VMEM((rows, wide), bf16),
            pltpu.VMEM((rows, wide), f32),
            pltpu.VMEM((rows, wide), f32),
            pltpu.VMEM((n_batch, 8, wide), f32),
            pltpu.VMEM((n_batch, 8, wide), f32),
            pltpu.SemaphoreType.DMA,
        ]
        + [pltpu.SemaphoreType.DMA((n_batch,))] * 4,
        compiler_params=pltpu.CompilerParams(
            collective_id=collective_id, has_side_effects=True, vmem_limit_bytes=62 * 2**20
        ),
        name="late_layer",
    )(raw, vectors, late_vectors, w_late, cotangent)


def backward_kernel(n_sec, n_chan, n_batch, act_ref, gh_ref, vec_ref, w_hbm, raw_hbm, x_hbm,
                    late_ref, early_ref, w_ref, raw_ref, x_ref, give, held, gact, buf,
                    fa, fb, sa, sb, part, pair, mine, low, high, last, square,
                    load_sem, put_sem, p1s, p1r, fas, far, fbs, fbr, sas, sar, sbs, sbr,
                    cas, car, cbs, cbr, p5s, p5r, sum_send, sum_recv,
                    pair_send, pair_recv, low_send, low_recv, high_send, high_recv,
                    last_send, last_recv):
    s, z, b = lax.axis_index("section"), lax.axis_index("chan"), lax.axis_index("batch")
    n_y = n_batch // 2
    y, core = b // 2, lax.rem(b, 2)
    sibling = {"batch": y * 2 + 1 - core}
    plane = [
        (lax.rem(s + i, n_sec), lax.rem(y + j, n_y))
        for i in range(n_sec) for j in range(n_y) if i + j > 0
    ]
    inner = [
        (lax.rem(s + i, n_sec), lax.rem(y + j, n_y))
        for i in range(1, n_sec) for j in range(1, n_y)
    ]
    loads = [
        pltpu.make_async_copy(w_hbm, w_ref, load_sem.at[0]),
        pltpu.make_async_copy(raw_hbm, raw_ref, load_sem.at[1]),
        pltpu.make_async_copy(x_hbm, x_ref, load_sem.at[2]),
    ]
    for load in loads:
        load.start()
    meet([{"batch": p} for p in others("batch", n_batch)]
         + [{"chan": p} for p in others("chan", n_chan)]
         + [{"section": p} for p in others("section", n_sec)]
         + [{"section": p, "batch": q * 2 + core} for p, q in inner])

    f32, bf16 = jnp.float32, jnp.bfloat16
    images, mid = act_ref.shape
    wide = gh_ref.shape[1]
    chunk = mid // CHUNKS
    half, tall = chunk // 2, chunk // 4
    step = min(wide, 512)

    def dev_sec(p):
        return {"section": p}

    def dev_y(q):
        return {"batch": q * 2 + core}

    kinds = [
        (n_sec, s, dev_sec, n_y, y, dev_y, fa, sa, fas, far, sas, sar, cas, car),
        (n_y, y, dev_y, n_sec, s, dev_sec, fb, sb, fbs, fbr, sbs, sbr, cbs, cbr),
    ]

    def span_of(k, t, p):
        sub = tall // kinds[t][0]
        return pl.ds(pl.multiple_of(k * chunk + core * half + t * tall + p * sub, sub), sub)

    def to_pair(k):
        return remote(give.at[k], held.at[k], p1s.at[k], p1r.at[k], sibling)

    def first(k, t, p, slot):
        n1, me, dev, _, _, _, buf1, _, ss, rs = kinds[t][:10]
        sub = tall // n1
        return remote(held.at[k, pl.ds(pl.multiple_of(t * tall + p * sub, sub), sub)],
                      buf1.at[k, slot], ss.at[k * n1 + p], rs.at[k * n1 + slot], dev(p))

    def second(k, t, q, slot):
        _, _, _, n2, me, dev, _, buf2, _, _, ss, rs = kinds[t][:12]
        return remote(buf2.at[k, me], buf2.at[k, slot], ss.at[k * n2 + q], rs.at[k * n2 + slot], dev(q))

    def third(k, t, p, slot):
        n1, me, dev, _, _, _, buf1 = kinds[t][:7]
        ss, rs = kinds[t][12:]
        return remote(buf1.at[k, me], late_ref.at[span_of(k, t, slot)], ss.at[k * n1 + p],
                      rs.at[k * n1 + slot], dev(p))

    def keep(k, t):
        me, buf1 = kinds[t][1], kinds[t][6]
        return pltpu.make_async_copy(buf1.at[k, me], late_ref.at[span_of(k, t, me)],
                                     put_sem.at[k * 2 + t])

    def share(k, which):
        rows = pl.ds(pl.multiple_of(k * chunk + which * half, half), half)
        return remote(late_ref.at[rows], late_ref.at[rows], p5s.at[k], p5r.at[k], sibling)

    def peers_of(n, me):
        return [lax.rem(me + d, n) for d in range(1, n)]

    def product(k):
        def run(which, dst, add):
            start = pl.multiple_of(k * chunk + which * half, half)
            lhs = act_ref[:, pl.ds(start, half)].T

            @pl.loop(0, wide // step)
            def _(i):
                cols = pl.ds(pl.multiple_of(i * step, step), step)
                block = jnp.dot(lhs, gh_ref[:, cols], preferred_element_type=f32)
                if add:
                    block = block + dst[k, :, cols].astype(f32)
                dst[k, :, cols] = block.astype(bf16)

        run(1 - core, give, False)
        to_pair(k).start()
        return run

    def own_product(k, run):
        to_pair(k).wait_recv()
        run(core, held, True)
        for t in range(2):
            n1, me = kinds[t][:2]
            for p in peers_of(n1, me):
                first(k, t, p, me).start()

    waiting = None
    for k in range(CHUNKS):
        run = product(k)
        if waiting is not None:
            own_product(k - 1, waiting)
        waiting = run
    own_product(CHUNKS - 1, waiting)

    def scatter_done(k):
        for t in range(2):
            n1, me, _, n2, me2, _, buf1, buf2 = kinds[t][:8]
            sub = tall // n1
            total = held[k, pl.ds(pl.multiple_of(t * tall + me * sub, sub), sub)].astype(f32)
            for p in peers_of(n1, me):
                first(k, t, p, p).wait_recv()
                total = total + buf1[k, p].astype(f32)
            buf2[k, me2] = total.astype(bf16)
            for q in peers_of(n2, me2):
                second(k, t, q, me2).start()

    def sum_done(k):
        for t in range(2):
            n1, me, _, n2, me2, _, buf1, buf2 = kinds[t][:8]
            for q in peers_of(n2, me2):
                second(k, t, q, q).wait_recv()
            total = buf2[k, 0].astype(f32)
            for j in range(1, n2):
                total = total + buf2[k, j].astype(f32)
            buf1[k, me] = total.astype(bf16)
            for p in peers_of(n1, me):
                third(k, t, p, me).start()
            keep(k, t).start()

    def gather_done(k):
        for t in range(2):
            n1, me = kinds[t][:2]
            for p in peers_of(n1, me):
                third(k, t, p, p).wait_recv()
            keep(k, t).wait()
        share(k, core).start()

    for load in loads:
        load.wait()
    buf[b] = jnp.zeros(buf.shape[1:], f32)
    lane = 256
    tile = 512

    def chain(i):
        cols = pl.ds(pl.multiple_of(i * lane, lane), lane)
        mean, rstd = vec_ref[0:1, cols], vec_ref[1:2, cols]
        gain, bias = vec_ref[2:3, cols], vec_ref[3:4, cols]

        @pl.loop(0, images // tile)
        def _(j):
            rows = pl.ds(pl.multiple_of(j * tile, tile), tile)
            square[...] = lax.dot_general(
                gh_ref[rows, :], w_ref[cols, :], (((1,), (1,)), ((), ())),
                preferred_element_type=f32,
            )

            def strip(r, sums):
                here = pl.ds(pl.multiple_of(j * tile + r * STRIP, STRIP), STRIP)
                normed = (raw_ref[here, cols].astype(f32) - mean) * rstd
                pre = normed * gain + bias
                gate = half_gate(pre)
                grad = square[pl.ds(pl.multiple_of(r * STRIP, STRIP), STRIP), :]
                grad = grad * (gate * (1.0 + pre * (1.0 - gate)))
                gact[here, cols] = grad.astype(bf16)
                return sums[0] + fold(grad), sums[1] + fold(grad * normed)

            zero = jnp.zeros((8, lane), f32)
            one, two = lax.fori_loop(0, tile // STRIP, strip, (zero, zero), unroll=2)
            buf[b, 0:1, cols] += jnp.sum(one, 0, keepdims=True)
            buf[b, 1:2, cols] += jnp.sum(two, 0, keepdims=True)

    tiles = mid // lane
    for k in range(CHUNKS):
        @pl.loop(k * tiles // CHUNKS, (k + 1) * tiles // CHUNKS)
        def _(i):
            chain(i)

        scatter_done(k)

    sums = exchange(n_batch, buf, sum_send, sum_recv)
    count = images * n_batch
    buf[b] = sums / count

    @pl.loop(0, mid // lane)
    def _(i):
        cols = pl.ds(pl.multiple_of(i * lane, lane), lane)
        mean, rstd, gain = vec_ref[0:1, cols], vec_ref[1:2, cols], vec_ref[2:3, cols]
        one, two = buf[b, 0:1, cols], buf[b, 1:2, cols]

        @pl.loop(0, images // STRIP)
        def _(j):
            rows = pl.ds(pl.multiple_of(j * STRIP, STRIP), STRIP)
            normed = (raw_ref[rows, cols].astype(f32) - mean) * rstd
            grad = gact[rows, cols].astype(f32)
            gact[rows, cols] = (gain * rstd * (grad - one - normed * two)).astype(bf16)

    rows, width = early_ref.shape
    span = rows * n_batch
    step_e = min(width, 512)
    order = []
    for i in range(n_chan // 2):
        order += [i, n_chan - 1 - i]

    def early_part(d):
        lhs = jnp.concatenate(
            [x_ref[:, (k * n_chan + d) * span:(k * n_chan + d + 1) * span] for k in range(n_sec)], 1
        ).T

        @pl.loop(0, width // step_e)
        def _(i):
            cols = pl.ds(pl.multiple_of(i * step_e, step_e), step_e)
            block = jnp.dot(lhs, gact[:, cols], preferred_element_type=f32)
            part[d, :, :, :, :, cols] = block.reshape(n_sec, n_y, 2, rows, step_e).astype(bf16)

        pair_copy(d).start()

    def pair_copy(d):
        return remote(part.at[d, :, :, 1 - core], pair.at[d], pair_send.at[d], pair_recv.at[d], sibling)

    def from_pair(d):
        pair_copy(d).wait_recv()
        mine[d] = (part[d, :, :, core].astype(f32) + pair[d].astype(f32)).astype(bf16)

    def lower(d):
        return remote(mine.at[d], low.at[d], low_send.at[d], low_recv.at[d],
                      {"chan": lax.rem(z + n_chan - 1, n_chan)})

    def upper(d):
        return remote(mine.at[d], high.at[d], high_send.at[d], high_recv.at[d],
                      {"chan": lax.rem(z + 1, n_chan)})

    def add(d, arrived):
        mine[d] = (mine[d].astype(f32) + arrived[d].astype(f32)).astype(bf16)

    def ready(d):
        from_pair(d)

        @pl.when(jnp.logical_and(z == n_chan - 1, d < z))
        def _():
            lower(d).start()

        @pl.when(jnp.logical_and(z == 0, d > z))
        def _():
            upper(d).start()

    for n, d in enumerate(order):
        early_part(d)
        if n > 0:
            ready(order[n - 1])
        if n == 0 or n == 2:
            sum_done(n // 2)
    ready(order[-1])
    for k in range(2, CHUNKS):
        sum_done(k)

    later = [lambda k=k: gather_done(k) for k in range(CHUNKS)]
    for i in range(n_chan):
        d, e = i, n_chan - 1 - i

        @pl.when(jnp.logical_and(z < n_chan - 1, d <= z))
        def _():
            lower(d).wait_recv()
            add(d, low)

            @pl.when(d < z)
            def _():
                lower(d).start()

        @pl.when(jnp.logical_and(z > 0, e >= z))
        def _():
            upper(e).wait_recv()
            add(e, high)

            @pl.when(e > z)
            def _():
                upper(e).start()

        if i < 2:
            for act_now in later[:2]:
                act_now()
            later = later[2:]

    slot = s * n_y + y
    for p, q in plane:
        remote(mine.at[z, p, q], last.at[slot], last_send.at[p * n_y + q], last_recv.at[slot],
               {"section": p, "batch": q * 2 + core}).start()
    for act_now in later:
        act_now()
    total = mine[z, s, y].astype(f32)
    for p, q in plane:
        there = p * n_y + q
        remote(mine.at[z, p, q], last.at[there], last_send.at[there], last_recv.at[there],
               {"section": p, "batch": q * 2 + core}).wait()
        total = total + last[there].astype(f32)
    early_ref[...] = total
    for d in range(n_chan):
        pair_copy(d).wait_send()

        @pl.when(d < z)
        def _():
            lower(d).wait_send()

        @pl.when(d > z)
        def _():
            upper(d).wait_send()

    for k in range(CHUNKS):
        share(k, 1 - core).wait_recv()
        share(k, core).wait_send()
        to_pair(k).wait_send()
        for t in range(2):
            n1, me, _, n2, me2 = kinds[t][:5]
            for p in peers_of(n1, me):
                first(k, t, p, me).wait_send()
                third(k, t, p, me).wait_send()
            for q in peers_of(n2, me2):
                second(k, t, q, me2).wait_send()


def backward(act, grad_h, vectors, w_late, raw, x, collective_id):
    n_sec, n_chan, n_batch = (lax.axis_size(a) for a in ("section", "chan", "batch"))
    n_y = n_batch // 2
    mid, wide = w_late.shape
    rows = x.shape[1] // (n_sec * n_chan * n_batch)
    quarter = (n_chan, n_sec, n_y, rows, mid)
    half, tall = mid // CHUNKS // 2, mid // CHUNKS // 4
    bf16 = jnp.bfloat16
    vmem, anywhere = pl.BlockSpec(memory_space=pltpu.VMEM), pl.BlockSpec(memory_space=pl.ANY)
    sems = [3, 2 * CHUNKS, CHUNKS, CHUNKS]
    sems += [CHUNKS * n for n in (n_sec, n_sec, n_y, n_y, n_y, n_y, n_sec, n_sec, n_sec, n_sec, n_y, n_y)]
    sems += [CHUNKS, CHUNKS, n_batch, n_batch] + [n_chan] * 6 + [n_sec * n_y] * 2
    return pl.pallas_call(
        functools.partial(backward_kernel, n_sec, n_chan, n_batch),
        out_shape=(
            jax.ShapeDtypeStruct((mid, wide), bf16),
            jax.ShapeDtypeStruct((rows, mid), jnp.float32),
        ),
        in_specs=[vmem, vmem, vmem, anywhere, anywhere, anywhere],
        out_specs=[anywhere, vmem],
        scratch_shapes=[
            pltpu.VMEM(w_late.shape, bf16),
            pltpu.VMEM(raw.shape, bf16),
            pltpu.VMEM(x.shape, bf16),
            pltpu.VMEM((CHUNKS, half, wide), bf16),
            pltpu.VMEM((CHUNKS, half, wide), bf16),
            pltpu.VMEM(raw.shape, bf16),
            pltpu.VMEM((n_batch, 8, mid), jnp.float32),
            pltpu.VMEM((CHUNKS, n_sec, tall // n_sec, wide), bf16),
            pltpu.VMEM((CHUNKS, n_y, tall // n_y, wide), bf16),
            pltpu.VMEM((CHUNKS, n_y, tall // n_sec, wide), bf16),
            pltpu.VMEM((CHUNKS, n_sec, tall // n_y, wide), bf16),
            pltpu.VMEM((n_chan, n_sec, n_y, 2, rows, mid), bf16),
        ]
        + [pltpu.VMEM(quarter, bf16)] * 4
        + [pltpu.VMEM((n_sec * n_y, rows, mid), bf16), pltpu.VMEM((512, 256), jnp.float32)]
        + [pltpu.SemaphoreType.DMA((n,)) for n in sems],
        compiler_params=pltpu.CompilerParams(
            collective_id=collective_id, has_side_effects=True, vmem_limit_bytes=63 * 2**20
        ),
        name="backward",
    )(act, grad_h, vectors, w_late, raw, x)


def body(images, w_early, gain_early, bias_early, w_late, gain_late, bias_late, cotangent):
    width_in = images.shape[-1]
    width_out = w_late.shape[1]
    batch_count = lax.axis_size("batch")
    own = images.reshape(-1, width_in)
    flat_in, raw, sums_e = early_forward(own, w_early, 0)
    total_rows = flat_in.shape[0] * batch_count

    mean_e = sums_e[0] / total_rows
    rstd_e = lax.rsqrt(sums_e[1] / total_rows - mean_e * mean_e + 1e-05)
    vectors = jnp.pad(jnp.stack([mean_e, rstd_e, gain_early, bias_early]), ((0, 4), (0, 0)))
    late_vectors = jnp.pad(jnp.stack([gain_late, bias_late]), ((0, 6), (0, 0)))
    act, late_out, grad_h = late_layer(
        raw, vectors, late_vectors, w_late, cotangent.reshape(-1, width_out), 1
    )
    late_out = late_out.reshape(cotangent.shape)

    grad_late, grad_early = backward(act, grad_h, vectors, w_late, raw, flat_in, 4)
    grad_late = grad_late.astype(jnp.float32)
    return (late_out, grad_late, grad_early)


def solution(mesh):
    return jax.shard_map(
        body,
        mesh=mesh,
        in_specs=(
            P("section", "batch", "chan", None, None),
            P(),
            P(),
            P(),
            P(None, "chan"),
            P("chan"),
            P("chan"),
            P("section", "batch", None, "chan"),
        ),
        out_specs=(
            P("section", "batch", None, "chan"),
            P(None, "chan"),
            P(("section", "chan", "batch"), None),
        ),
        check_vma=False,
    )
```
